512 devices in a mesh: row: 16 (over y, z_hi), col: 32 (over x, z_lo, core).
Axes of the slice: x: 4, y: 4, z: 16 (z_hi: 4, z_lo: 4; z = z_hi * 4 + z_lo), core: 2. Of those that a mesh axis runs over, the one named last changes fastest.
Arguments:
- positions: float32 [3, 524288], P(None, ('row', 'col')), may hold values from 0 to 1
- strengths: float32 [3, 524288], P(None, ('row', 'col')), may hold values from -0.06 to 0.06
- radii: float32 [524288], P(('row', 'col')), may hold values from 0.1 to 0.3
- pair_list: int32 [2, 16, 32, 2], P(None, 'row', 'col'), may hold values from 0 to 31, as said below
- pair_count: int32 [16, 32], P('row', 'col'), may hold values from 1 to 2, as said below
Outputs:
- velocity: float32 [3, 524288], P(None, ('row', 'col'))
- stretching: float32 [3, 524288], P(None, ('row', 'col'))
The draws below stay inside these ranges and needn't reach their ends.
Inputs may be any that keep to these rules, and one draw needn't show every extreme that they name: `pair_list`: row-block indices lie in 0 to 31, column-block indices in 0 to 15; slot 0 of every tile pairs a group with itself. `pair_count`: some tile fills all 2 slots.
All inputs are finite; a program needn't handle non-finite values.
Results may differ from the reference program's by a relative error of at most 0.0003.
Values sent between devices are 32-bit elements; how exact they have to be, the bound alone decides.
A program may use at most 192 MiB of HBM per device.

```python
import math
import jax
import jax.numpy as jnp
from jax import lax

G = 1024
GD = 1
PMAX = 2
NP = 524288
N_ROW = 16
N_COL = 32


def draw_pair_list(key, part):
    key = jax.random.fold_in(key, 11)
    k_row, k_col, k_diag = jax.random.split(key, 3)
    rows_part = jax.random.randint(k_row, (N_ROW, N_COL, PMAX), 0, GD * N_COL)
    cols_part = jax.random.randint(k_col, (N_ROW, N_COL, PMAX), 0, GD * N_ROW)
    offset = jax.random.randint(k_diag, (N_ROW, N_COL), 0, GD)
    rows_i = jnp.arange(N_ROW, dtype=jnp.int32)[:, None]
    cols_i = jnp.arange(N_COL, dtype=jnp.int32)[None, :]
    rows_part = rows_part.at[:, :, 0].set(cols_i * GD + offset)
    cols_part = cols_part.at[:, :, 0].set(rows_i * GD + offset)
    return jnp.stack([rows_part, cols_part]).astype(jnp.int32)


def draw_pair_count(key, part):
    key = jax.random.fold_in(key, 23)
    k_base, k_full = jax.random.split(key, 2)
    lowest = max(1, (PMAX + 1) // 2)
    counts = jax.random.randint(k_base, (N_ROW * N_COL,), lowest, PMAX + 1)
    full = jax.random.randint(k_full, (), 0, N_ROW * N_COL)
    counts = counts.at[full].set(PMAX)
    return counts.reshape(N_ROW, N_COL).astype(jnp.int32)


def block_scale(own_key, extent, pieces, least, top_value):
    def one(axis_at, shards_of):
        steps = jax.random.uniform(jax.random.fold_in(jax.random.fold_in(own_key, 6), axis_at), (shards_of,), jnp.float32, least / len(pieces), top_value / len(pieces))
        return jnp.repeat(jnp.exp(steps), extent[axis_at] // shards_of).reshape((-1,) + (1,) * (len(extent) - axis_at - 1))

    factor_of = one(*pieces[0])
    for cut in pieces[1:]:
        factor_of = factor_of * one(*cut)
    return factor_of


def centred(stream_key, dims, scale, most, cuts=(), kind=jnp.bfloat16):
    values = jax.random.normal(stream_key, dims, jnp.float32) * scale
    if len(cuts) > 0:
        values = block_scale(stream_key, dims, cuts, -0.22, 0.18) * values
    return jnp.clip(values, min=-most, max=most).astype(kind)


def setup_inputs(seed: int = 0) -> dict:
    seeds = jax.random.split(jax.random.key(seed), 6)
    return {
        "positions": jnp.clip(1.0 * jax.random.uniform(seeds[0], (3, NP), jnp.float32) ** block_scale(seeds[0], (3, NP), ((1, 512),), -0.2, 0.2), 0.0, 1.0),
        "strengths": centred(seeds[1], (3, NP), 0.01, 0.06, ((1, 512),), jnp.float32),
        "radii": jnp.clip(jnp.exp(math.log(0.3) - 1.0986123 * jax.random.uniform(seeds[2], (NP,), jnp.float32) ** block_scale(seeds[2], (NP,), ((0, 512),), -0.2, 0.2)), 0.1, 0.3),
        "pair_list": draw_pair_list(jax.random.fold_in(seeds[5], 71), 0),
        "pair_count": draw_pair_count(jax.random.fold_in(seeds[5], 71), 0),
    }


def cross_rows(u_a, u_b):
    return jnp.stack([u_a[1] * u_b[2] - u_a[2] * u_b[1], u_a[2] * u_b[0] - u_a[0] * u_b[2], u_a[0] * u_b[1] - u_a[1] * u_b[0]])


def pair_terms(pos_a, str_a, rad_a, pos_b, str_b, rad_b):
    rvec = pos_a[:, :, None] - pos_b[:, None, :]
    rho = jnp.sum(rvec * rvec, axis=0)
    spread = 0.5 * (rad_a[:, None] ** 2 + rad_b[None, :] ** 2)
    inner = rho + spread
    power = inner ** -2.5
    upper = rho + 2.5 * spread
    kern = upper * power
    slope = 2.0 * (power - 2.5 * upper * power / inner)
    scale = 1.0 / (4.0 * jnp.pi)
    sa = str_a[:, :, None]
    sb = str_b[:, None, :]
    r_x_b = cross_rows(rvec, sb)
    r_x_a = cross_rows(rvec, sa)
    a_x_b = cross_rows(sa, sb)
    dot_a = jnp.sum(sa * rvec, axis=0)
    dot_b = jnp.sum(sb * rvec, axis=0)
    vel_a = -scale * jnp.sum(kern * r_x_b, axis=2)
    vel_b = scale * jnp.sum(kern * r_x_a, axis=1)
    str_ta = -scale * jnp.sum(kern * a_x_b + slope * dot_a * r_x_b, axis=2)
    str_tb = -scale * jnp.sum(-kern * a_x_b + slope * dot_b * r_x_a, axis=1)
    return jnp.concatenate([vel_a, str_ta]), jnp.concatenate([vel_b, str_tb])


def reference(positions, strengths, radii, pair_list, pair_count):
    rows_i = jnp.arange(N_ROW, dtype=jnp.int32)[:, None, None]
    cols_i = jnp.arange(N_COL, dtype=jnp.int32)[None, :, None]
    slots = jnp.arange(PMAX, dtype=jnp.int32)[None, None, :]
    kk = pair_list[0]
    mm = pair_list[1]
    grp_a = (rows_i * N_COL + kk // GD) * GD + kk % GD
    grp_b = ((mm // GD) * N_COL + cols_i) * GD + mm % GD
    live = (slots < pair_count[:, :, None]).astype(jnp.int32)
    grp_a = grp_a.reshape(-1).astype(jnp.int32)
    grp_b = grp_b.reshape(-1).astype(jnp.int32)
    live = live.reshape(-1)
    total = jnp.zeros((6, positions.shape[1]), jnp.float32)

    def visit(acc, item):
        ga, gb, lv = item

        def work(acc_in):
            sa = (ga * G).astype(jnp.int32)
            sb = (gb * G).astype(jnp.int32)
            pa = lax.dynamic_slice_in_dim(positions, sa, G, 1)
            pb = lax.dynamic_slice_in_dim(positions, sb, G, 1)
            ta = lax.dynamic_slice_in_dim(strengths, sa, G, 1)
            tb = lax.dynamic_slice_in_dim(strengths, sb, G, 1)
            ra = lax.dynamic_slice_in_dim(radii, sa, G, 0)
            rb = lax.dynamic_slice_in_dim(radii, sb, G, 0)
            side_a, side_b = pair_terms(pa, ta, ra, pb, tb, rb)
            other = jnp.where(ga == gb, 0.0, 1.0).astype(jnp.float32)
            cur_a = lax.dynamic_slice_in_dim(acc_in, sa, G, 1)
            acc_in = lax.dynamic_update_slice_in_dim(acc_in, cur_a + side_a, sa, 1)
            cur_b = lax.dynamic_slice_in_dim(acc_in, sb, G, 1)
            return lax.dynamic_update_slice_in_dim(acc_in, cur_b + other * side_b, sb, 1)

        return lax.cond(lv > 0, work, lambda acc_in: acc_in, acc), None

    total, unused = lax.scan(visit, total, (grp_a, grp_b, live))
    return total[:3], total[3:]
```

```python
import functools
import math

import jax
import jax.numpy as jnp
from jax import lax
from jax.experimental import pallas as pl
from jax.experimental.pallas import tpu as pltpu
from jax.sharding import PartitionSpec as P

G = 1024
MESH = pl.DeviceIdType.MESH
f32, bf16 = jnp.float32, jnp.bfloat16
TI, TJ = 512, 256

NY, NH, NX, NL, NC = 4, 4, 4, 4, 2
NEAR = [(dx, dc) for dx in range(NX) for dc in range(NC)]


def coords():
    r, c = lax.axis_index("row"), lax.axis_index("col")
    return r // NH, r % NH, c // (NL * NC), (c // NC) % NL, c % NC


def at(dy=0, dh=0, dx=0, dl=0, dc=0):
    y, h, x, l, c = coords()
    row = ((y + dy) % NY) * NH + (h + dh) % NH
    col = (((x + dx) % NX) * NL + (l + dl) % NL) * NC + (c + dc) % NC
    return {"row": row, "col": col}


def split3(v):
    h = v.astype(bf16).astype(f32)
    rest = v - h
    m = rest.astype(bf16).astype(f32)
    return h, m, rest - m


def cross(p, q):
    return [p[1] * q[2] - p[2] * q[1], p[2] * q[0] - p[0] * q[2], p[0] * q[1] - p[1] * q[0]]


def rows_of(v, n):
    return [v[i : i + 1] for i in range(n)]


def wide(ref, n):
    return jnp.concatenate([ref[pl.ds(s, n, stride=8), :] for s in range(8)], axis=1)


def narrow(ref, v, first, n):
    for s in range(8):
        ref[pl.ds(8 * first + s, n, stride=8), :] = v[:, s * 128 : (s + 1) * 128]


def metric(x, hs):
    n = x.shape[1]
    u = x[0:1] * x[0:1] + x[1:2] * x[1:2] + x[2:3] * x[2:3] + hs
    one, zero = jnp.ones((1, n), f32), jnp.zeros((3, n), f32)
    lh, lm, ll = split3(jnp.concatenate([-2.0 * x, u, one, zero], 0))
    rh, rm, rl = split3(jnp.concatenate([x, one, u, zero], 0))
    left = jnp.concatenate([lh, lh, lm, lm, lh, ll], 0).astype(bf16)
    right = jnp.concatenate([rh, rm, rh, rm, rl, rh], 0).astype(bf16)
    return left, right


def moments(x, al):
    e = jnp.concatenate([al] + cross(rows_of(x, 3), rows_of(al, 3)) + [jnp.zeros((2, x.shape[1]), f32)], 0)
    f = jnp.concatenate([e, x[0:1] * e, x[1:2] * e, x[2:3] * e], 0)
    return jnp.concatenate(split3(e), 0).astype(bf16), jnp.concatenate(split3(f), 0).astype(bf16)


def finish(x, al, sg, sh):
    xs, a = rows_of(x, 3), rows_of(al, 3)
    g0, g1 = rows_of(sg[0:3], 3), rows_of(sg[3:6], 3)
    sh = -5.0 * sh
    row = lambda p, q: sh[8 * p + q : 8 * p + q + 1]
    h0, h1 = [row(0, q) for q in range(3)], [row(0, 3 + q) for q in range(3)]
    at0 = [a[0] * row(1, q) + a[1] * row(2, q) + a[2] * row(3, q) for q in range(3)]
    at1 = [a[0] * row(1, 3 + q) + a[1] * row(2, 3 + q) + a[2] * row(3, 3 + q) for q in range(3)]
    ax = a[0] * xs[0] + a[1] * xs[1] + a[2] * xs[2]
    c0, c1, c2, c3 = cross(xs, g0), cross(xs, h0), cross(xs, at0), cross(a, g0)
    scale = 1.0 / (4.0 * math.pi)
    vel = [scale * (g1[i] - c0[i]) for i in range(3)]
    stretch = [-scale * (c3[i] + ax * (c1[i] - h1[i]) - c2[i] + at1[i]) for i in range(3)]
    return jnp.concatenate(vel + stretch, 0)


def dot(a, b, dims):
    return lax.dot_general(a, b, (dims, ((), ())), preferred_element_type=f32)


def halves(v):
    h = v.astype(bf16)
    return h, (v - h.astype(f32)).astype(bf16)


def kernels_of(left, right, si, sj):
    y = lax.rsqrt(dot(left, right, ((0,), (0,))))
    y2 = y * y
    p = y2 * y
    t = (si + sj) * y2
    return halves(p + p * t) + halves((p * y2) * (0.6 + t))


def fold(hi, lo, n):
    return (hi[:n] + hi[n : 2 * n] + hi[2 * n :]) + (lo[:n] + lo[n:])


def column(hs):
    return jnp.transpose(jnp.broadcast_to(hs, (128, G)))


def kernel(pos, stg, rad, plist, pcount, vel, stretch,
           own, req, zhb, zlb, reqy, reqn, asend, arecv, bsend, brecv, pa, pb,
           yrecv, hsend, hrecv, nrecv, lsend, lrecv, aop, bop,
           left, right, col, rowj, ea, fa, eb, fb, sga, sha, sgb, shb, sout,
           ssem, rsem):
    y, h, x, l, c = coords()
    bar = pltpu.get_barrier_semaphore()
    peers = (
        [dict(dh=1), dict(dh=3)]
        + [dict(dy=d) for d in (1, 2, 3)]
        + [dict(dl=d) for d in (1, 2, 3)]
        + [dict(dx=dx, dc=dc) for dx, dc in NEAR[1:]]
    )
    for o in peers:
        pl.semaphore_signal(bar, inc=1, device_id=at(**o), device_id_type=MESH)

    used = [0]

    def send(src, dst, **o):
        i = used[0]
        used[0] += 1
        cp = pltpu.make_async_remote_copy(
            src_ref=src, dst_ref=dst, send_sem=ssem.at[i], recv_sem=rsem.at[i],
            device_id=at(**o), device_id_type=MESH)
        cp.start()
        return cp

    sent = []
    narrow(own, pos[...], 0, 3)
    narrow(own, stg[...], 3, 3)
    own[48:56, :] = rad[...]
    k, m, live = plist[0, 0, 0, 1], plist[1, 0, 0, 1], (pcount[0, 0] > 1).astype(jnp.int32)
    ri = lax.broadcasted_iota(jnp.int32, (8, 128), 0)
    req[...] = jnp.where(ri == 0, k, jnp.where(ri == 1, m, live))

    own_x, own_al, own_r = wide(own, 7)[0:3], wide(own, 7)[3:6], wide(own, 7)[6:7]
    own_x = own_x - jnp.mean(own_x, axis=1, keepdims=True)
    own_hs = 0.5 * own_r * own_r
    left[...], right[...] = metric(own_x, own_hs)
    ea[...], fa[...] = moments(own_x, own_al)
    rowj[...] = 1.5 * own_hs
    col[...] = column(1.5 * own_hs)

    def block(i0, j0, two):
        si = jnp.concatenate([col[pl.ds(i0, TI), :]] * (TJ // 128), 1)
        gh, gl, hh, hl = kernels_of(left[:, pl.ds(i0, TI)], right[:, pl.ds(j0, TJ)], si, rowj[:, pl.ds(j0, TJ)])
        d = ((1,), (0,))
        ei, fi = ea[:, pl.ds(i0, TI)], fa[:, pl.ds(i0, TI)]
        sgb[:, pl.ds(j0, TJ)] += fold(dot(ei, gh, d), dot(ei[:16], gl, d), 8)
        shb[:, pl.ds(j0, TJ)] += fold(dot(fi, hh, d), dot(fi[:64], hl, d), 32)
        if two:
            d = ((1,), (1,))
            ej, fj = eb[:, pl.ds(j0, TJ)], fb[:, pl.ds(j0, TJ)]
            sga[:, pl.ds(i0, TI)] += fold(dot(ej, gh, d), dot(ej[:16], gl, d), 8)
            sha[:, pl.ds(i0, TI)] += fold(dot(fj, hh, d), dot(fj[:64], hl, d), 32)

    sgb[...] = jnp.zeros_like(sgb)
    shb[...] = jnp.zeros_like(shb)
    for j0 in range(0, G, TJ):
        block(0, j0, False)

    pl.semaphore_wait(bar, len(peers))

    zh_p = send(own, zhb.at[3], dh=1)
    zh_m = send(own, zhb.at[1], dh=3)
    to_l = [send(own, zlb.at[NL - d], dl=d) for d in (1, 2, 3)]
    to_n = [send(req, reqn.at[((NX - dx) % NX) * NC + dc], dx=dx, dc=dc) for dx, dc in NEAR[1:]]
    to_y = [send(req, reqy.at[NY - d], dy=d) for d in (1, 2, 3)]
    sent += [zh_p, zh_m] + to_l + to_n + to_y
    zhb[0] = own[...]
    zlb[0] = own[...]
    reqn[0] = req[...]
    reqy[0] = req[...]

    for cp in to_l + to_n + to_y:
        cp.wait_recv()

    def want(tile, r):
        return tile[r : r + 1, :]

    def pick(buf, index, n, first):
        out = buf[0]
        for d in range(1, n):
            out = jnp.where(index == (first + d) % n, buf[d], out)
        return out

    near = []
    for i, (dx, dc) in enumerate(NEAR):
        kk = want(reqn[i], 0)
        asend[i] = pick(zlb, (kk // NC) % NL, NL, l)
        if i:
            slot = ((NX - dx) % NX) * NC + dc
            near.append(send(asend.at[i], arecv.at[slot], dx=dx, dc=dc))
    sent += near
    arecv[0] = asend[0]

    zh_p.wait_recv()
    f_p = send(zhb.at[3, pl.ds(0, 24)], zhb.at[2, pl.ds(0, 24)], dh=1)
    zh_m.wait_recv()
    f_m = send(zhb.at[1, pl.ds(24, 32)], zhb.at[2, pl.ds(24, 32)], dh=3)
    sent += [f_p, f_m]

    for j0 in range(0, G, TJ):
        block(TI, j0, False)
    sout[...] = finish(own_x, own_al, sgb[...], shb[...])

    for cp in near:
        cp.wait_recv()
    kk = want(req[...], 0)
    a = arecv[0]
    for i, (dx, dc) in list(enumerate(NEAR))[1:]:
        hit = (kk // (NL * NC) == (x + dx) % NX) & (kk % NC == (c + dc) % NC)
        a = jnp.where(hit, arecv[i], a)
    aop[...] = a
    a7 = wide(aop, 7)
    centre = jnp.mean(a7[0:3], axis=1, keepdims=True)
    ax_, aal, ahs = a7[0:3] - centre, a7[3:6], 0.5 * a7[6:7] * a7[6:7]
    left[...] = metric(ax_, ahs)[0]
    ea[...], fa[...] = moments(ax_, aal)
    col[...] = column(1.5 * ahs)

    f_p.wait_recv()
    f_m.wait_recv()
    along = []
    for d in range(NY):
        mm = want(reqy[d], 1)
        bsend[d] = pick(zhb, mm % NH, NH, h)
        if d:
            along.append(send(bsend.at[d], brecv.at[NY - d], dy=d))
    sent += along
    brecv[0] = bsend[0]
    for cp in along:
        cp.wait_recv()
    mm = want(req[...], 1)
    bop[...] = pick(brecv, mm // NH, NY, y)
    b7 = wide(bop, 7)
    bx_, bal, bhs = b7[0:3] - centre, b7[3:6], 0.5 * b7[6:7] * b7[6:7]
    right[...] = metric(bx_, bhs)[1]
    eb[...], fb[...] = moments(bx_, bal)
    rowj[...] = 1.5 * bhs

    sgb[...] = jnp.zeros_like(sgb)
    shb[...] = jnp.zeros_like(shb)
    sga[...] = jnp.zeros_like(sga)
    sha[...] = jnp.zeros_like(sha)

    def slot1(jj, carry):
        j0 = pl.multiple_of(jj * TJ, TJ)
        for i0 in range(0, G, TI):
            block(i0, j0, True)
        return carry

    lax.fori_loop(0, G // TJ, slot1, 0)
    narrow(pb, finish(bx_, bal, sgb[...], shb[...]), 0, 6)
    back_y = [send(pb, yrecv.at[NY - d], dy=d) for d in (1, 2, 3)]
    yrecv[0] = pb[...]
    narrow(pa, finish(ax_, aal, sga[...], sha[...]), 0, 6)
    back_n = [
        send(pa, nrecv.at[((NX - dx) % NX) * NC + dc], dx=dx, dc=dc) for dx, dc in NEAR[1:]
    ]
    nrecv[0] = pa[...]
    sent += back_y + back_n

    for cp in back_y:
        cp.wait_recv()
    zero = jnp.zeros((48, 128), f32)
    bins = [zero] * NH
    for d in range(NY):
        t = reqy[d]
        kk, mm, on = want(t, 0), want(t, 1), want(t, 2)
        self_pair = (mm == ((y + d) % NY) * NH + h) & (kk == (x * NL + l) * NC + c)
        mine = (on == 1) & (mm // NH == y) & jnp.logical_not(self_pair)
        for e in range(NH):
            bins[e] = bins[e] + jnp.where(mine & (mm % NH == (h + e) % NH), yrecv[d], zero)
    back_h = []
    for e in (2, 1, 3):
        hsend[e] = bins[e]
        back_h.append(send(hsend.at[e], hrecv.at[NH - e], dh=e))
    sent += back_h

    for cp in back_n:
        cp.wait_recv()
    lbins = [zero] * NL
    for i in range(len(NEAR)):
        t = reqn[i]
        kk, on = want(t, 0), want(t, 2)
        mine = (on == 1) & (kk // (NL * NC) == x) & (kk % NC == c)
        for e in range(NL):
            lbins[e] = lbins[e] + jnp.where(mine & ((kk // NC) % NL == (l + e) % NL), nrecv[i], zero)
    back_l = []
    for e in (1, 2, 3):
        lsend[e] = lbins[e]
        back_l.append(send(lsend.at[e], lrecv.at[NL - e], dl=e))
    sent += back_l

    for cp in back_l + back_h:
        cp.wait_recv()
    total = bins[0] + lbins[0]
    for e in (1, 2, 3):
        total = total + lrecv[e] + hrecv[e]
    pa_total = aop
    pa_total[0:48, :] = total
    out = sout[...] + wide(pa_total, 6)
    vel[...] = out[0:3]
    stretch[...] = out[3:6]
    for cp in sent:
        cp.wait_send()
    assert used[0] == N_COPIES


N_COPIES = 2 + 3 + 7 + 3 + 7 + 2 + 3 + 3 + 7 + 3 + 3


def local(positions, strengths, radii, pair_list, pair_count):
    vm, sm = pl.BlockSpec(memory_space=pltpu.VMEM), pl.BlockSpec(memory_space=pltpu.SMEM)
    V = pltpu.VMEM
    out = jax.ShapeDtypeStruct((3, G), f32)
    item, part = (56, 128), (48, 128)
    return pl.pallas_call(
        kernel,
        out_shape=(out, out),
        in_specs=[vm, vm, vm, sm, sm],
        out_specs=(vm, vm),
        scratch_shapes=[
            V(item, f32), V((8, 128), jnp.int32), V((NH,) + item, f32), V((NL,) + item, f32),
            V((NY, 8, 128), jnp.int32), V((8, 8, 128), jnp.int32),
            V((8,) + item, f32), V((8,) + item, f32), V((NY,) + item, f32), V((NY,) + item, f32),
            V(part, f32), V(part, f32),
            V((NY,) + part, f32), V((NH,) + part, f32), V((NH,) + part, f32),
            V((8,) + part, f32), V((NL,) + part, f32), V((NL,) + part, f32),
            V(item, f32), V(item, f32),
            V((48, G), bf16), V((48, G), bf16), V((G, 128), f32), V((1, G), f32),
            V((24, G), bf16), V((96, G), bf16), V((24, G), bf16), V((96, G), bf16),
            V((8, G), f32), V((32, G), f32), V((8, G), f32), V((32, G), f32), V((6, G), f32),
            pltpu.SemaphoreType.DMA((N_COPIES,)), pltpu.SemaphoreType.DMA((N_COPIES,)),
        ],
        compiler_params=pltpu.CompilerParams(
            collective_id=0, has_side_effects=True, vmem_limit_bytes=48 * 2**20
        ),
        cost_estimate=pl.CostEstimate(flops=2 * G * G * 256, bytes_accessed=64 * G, transcendentals=2 * G * G),
        name="vortex_pairs",
    )(positions, strengths, radii.reshape(8, 128), pair_list, pair_count)


def solution(mesh):
    placed = (
        P(None, ("row", "col")),
        P(None, ("row", "col")),
        P(("row", "col")),
        P(None, "row", "col", None),
        P("row", "col"),
    )
    return jax.shard_map(
        local,
        mesh=mesh,
        in_specs=placed,
        out_specs=(P(None, ("row", "col")), P(None, ("row", "col"))),
        check_vma=False,
    )
```

```python
import functools
import math

import jax
import jax.numpy as jnp
from jax import lax
from jax.experimental import pallas as pl
from jax.experimental.pallas import tpu as pltpu
from jax.sharding import PartitionSpec as P

G = 1024
MESH = pl.DeviceIdType.MESH
f32, bf16 = jnp.float32, jnp.bfloat16
TJ = 256
NB = G // TJ

NY, NH, NX, NL, NC = 4, 4, 4, 4, 2
NEAR = [(dx, dc) for dx in range(NX) for dc in range(NC)]


def coords():
    r, c = lax.axis_index("row"), lax.axis_index("col")
    return r // NH, r % NH, c // (NL * NC), (c // NC) % NL, c % NC


def at(dy=0, dh=0, dx=0, dl=0, dc=0):
    y, h, x, l, c = coords()
    row = ((y + dy) % NY) * NH + (h + dh) % NH
    col = (((x + dx) % NX) * NL + (l + dl) % NL) * NC + (c + dc) % NC
    return {"row": row, "col": col}


def split3(v):
    h = v.astype(bf16).astype(f32)
    rest = v - h
    m = rest.astype(bf16).astype(f32)
    return h, m, rest - m


def cross(p, q):
    return [p[1] * q[2] - p[2] * q[1], p[2] * q[0] - p[0] * q[2], p[0] * q[1] - p[1] * q[0]]


def rows_of(v, n):
    return [v[i : i + 1] for i in range(n)]


def unpack(ref, half):
    return jnp.concatenate([ref[half, pl.ds(s, 7, stride=4), :] for s in range(4)], axis=1)


def pack(ref, k, v, first, step):
    n = v.shape[0]
    for s in range(step):
        ref[k, pl.ds(step * first + s, n, stride=step), :] = v[:, s * 128 : (s + 1) * 128]


def metric(x, hs):
    n = x.shape[1]
    u = x[0:1] * x[0:1] + x[1:2] * x[1:2] + x[2:3] * x[2:3] + hs
    one, zero = jnp.ones((1, n), f32), jnp.zeros((3, n), f32)
    lh, lm, ll = split3(jnp.concatenate([-2.0 * x, u, one, zero], 0))
    rh, rm, rl = split3(jnp.concatenate([x, one, u, zero], 0))
    left = jnp.concatenate([lh, lh, lm, lm, lh, ll], 0).astype(bf16)
    right = jnp.concatenate([rh, rm, rh, rm, rl, rh], 0).astype(bf16)
    return left, right


def moments(x, al):
    e = jnp.concatenate([al] + cross(rows_of(x, 3), rows_of(al, 3)) + [jnp.zeros((2, x.shape[1]), f32)], 0)
    f = jnp.concatenate([e, x[0:1] * e, x[1:2] * e, x[2:3] * e], 0)
    return jnp.concatenate(split3(e), 0).astype(bf16), jnp.concatenate(split3(f), 0).astype(bf16)


def finish(x, al, sg, sh):
    xs, a = rows_of(x, 3), rows_of(al, 3)
    g0, g1 = rows_of(sg[0:3], 3), rows_of(sg[3:6], 3)
    sh = -5.0 * sh
    row = lambda p, q: sh[8 * p + q : 8 * p + q + 1]
    h0, h1 = [row(0, q) for q in range(3)], [row(0, 3 + q) for q in range(3)]
    at0 = [a[0] * row(1, q) + a[1] * row(2, q) + a[2] * row(3, q) for q in range(3)]
    at1 = [a[0] * row(1, 3 + q) + a[1] * row(2, 3 + q) + a[2] * row(3, 3 + q) for q in range(3)]
    ax = a[0] * xs[0] + a[1] * xs[1] + a[2] * xs[2]
    c0, c1, c2, c3 = cross(xs, g0), cross(xs, h0), cross(xs, at0), cross(a, g0)
    scale = 1.0 / (4.0 * math.pi)
    vel = [scale * (g1[i] - c0[i]) for i in range(3)]
    stretch = [-scale * (c3[i] + ax * (c1[i] - h1[i]) - c2[i] + at1[i]) for i in range(3)]
    return jnp.concatenate(vel + stretch, 0)


def dot(a, b, dims):
    return lax.dot_general(a, b, (dims, ((), ())), preferred_element_type=f32)


def halves(v):
    h = v.astype(bf16)
    return h, (v - h.astype(f32)).astype(bf16)


def kernels_of(left, right, si, sj):
    y = lax.rsqrt(dot(left, right, ((0,), (0,))))
    y2 = y * y
    p = y2 * y
    t = (si + sj) * y2
    return halves(p + p * t) + halves((p * y2) * (0.6 + t))


def fold(hi, lo, n):
    return (hi[:n] + hi[n : 2 * n] + hi[2 * n :]) + (lo[:n] + lo[n:])


def column(hs):
    return jnp.transpose(jnp.broadcast_to(hs, (128, hs.shape[1])))


def kernel(pos_in, stg_in, rad_in, plist, pcount, result,
           pos, stg, rad, own, req, zhb, reqy, reql, nb, lsel, lrecv, bsend, brecv, aop, bop,
           pb, yrecv, hsend, hrecv, pa, lback, nsend, nrecv,
           left, right, col, rowj, ea, fa, eb, fb, sga, sha, sout, lsem, ssem, rsem):
    y, h, x, l, c = coords()
    bar = pltpu.get_barrier_semaphore()
    peers = (
        [dict(dh=1), dict(dh=3)]
        + [dict(dx=dx, dc=dc) for dx, dc in NEAR[1:]]
        + [dict(dl=d) for d in (1, 2, 3)]
        + [dict(dy=d) for d in (1, 2, 3)]
    )
    for o in peers:
        pl.semaphore_signal(bar, inc=1, device_id=at(**o), device_id_type=MESH)
    loads = [
        pltpu.make_async_copy(src, dst, lsem.at[i])
        for i, (src, dst) in enumerate([(pos_in, pos), (stg_in, stg), (rad_in, rad)])
    ]
    for cp in loads:
        cp.start()

    used = [0]
    sent = []

    def send(src, dst, **o):
        i = used[0]
        used[0] += 1
        cp = pltpu.make_async_remote_copy(
            src_ref=src, dst_ref=dst, send_sem=ssem.at[i], recv_sem=rsem.at[i],
            device_id=at(**o), device_id_type=MESH)
        cp.start()
        sent.append(cp)
        return cp

    k, m, live = plist[0, 0, 0, 1], plist[1, 0, 0, 1], (pcount[0, 0] > 1).astype(jnp.int32)
    ri = lax.broadcasted_iota(jnp.int32, (8, 128), 0)
    req[...] = jnp.where(ri == 0, k, jnp.where(ri == 1, m, live))
    for cp in loads:
        cp.wait()
    for half in range(2):
        part = slice(512 * half, 512 * half + 512)
        pack(own, half, pos[:, part], 0, 4)
        pack(own, half, stg[:, part], 3, 4)
        own[half, 24:28, :] = rad[4 * half : 4 * half + 4, :]

    item = jnp.concatenate([unpack(own, 0), unpack(own, 1)], axis=1)
    own_x, own_al, own_r = item[0:3], item[3:6], item[6:7]
    own_x = own_x - jnp.mean(own_x, axis=1, keepdims=True)
    own_hs = 0.5 * own_r * own_r
    left[...], right[...] = metric(own_x, own_hs)
    ea[...], fa[...] = moments(own_x, own_al)
    rowj[...] = 1.5 * own_hs
    col[...] = column(1.5 * own_hs)

    def block(q, two):
        js = pl.ds(q * TJ, TJ)
        si = jnp.concatenate([col[...]] * (TJ // 128), 1)
        gh, gl, hh, hl = kernels_of(left[...], right[:, js], si, rowj[:, js])
        d = ((1,), (0,))
        sg = fold(dot(ea[...], gh, d), dot(ea[:16], gl, d), 8)
        sh = fold(dot(fa[...], hh, d), dot(fa[:64], hl, d), 32)
        if two:
            d = ((1,), (1,))
            ej, fj = eb[:, js], fb[:, js]
            ag = fold(dot(ej, gh, d), dot(ej[:16], gl, d), 8)
            ah = fold(dot(fj, hh, d), dot(fj[:64], hl, d), 32)
            sga[...] = ag if q == 0 else sga[...] + ag
            sha[...] = ah if q == 0 else sha[...] + ah
        return sg, sh

    def own_block(q):
        js = slice(q * TJ, q * TJ + TJ)
        sout[:, js] = finish(own_x[:, js], own_al[:, js], *block(q, False))

    own_block(0)
    own_block(1)
    pl.semaphore_wait(bar, len(peers))

    zh_p = [send(own.at[0], zhb.at[3, 0], dh=1), None]
    zh_m = [None, send(own.at[1], zhb.at[1, 1], dh=3)]
    zh_p[1] = send(own.at[1], zhb.at[3, 1], dh=1)
    zh_m[0] = send(own.at[0], zhb.at[1, 0], dh=3)

    def near_slot(dx, dc):
        return ((NX - dx) % NX) * NC + dc

    near = [send(own, nb.at[near_slot(dx, dc)], dx=dx, dc=dc) for dx, dc in NEAR[1:]]
    ask = [send(req, reql.at[NL - d], dl=d) for d in (1, 2, 3)]
    ask += [send(req, reqy.at[NY - d], dy=d) for d in (1, 2, 3)]
    zhb[0] = own[...]
    nb[0] = own[...]
    reql[0] = req[...]
    reqy[0] = req[...]
    own_block(2)
    own_block(3)

    zh_p[0].wait_recv()
    f_p = send(zhb.at[3, 0], zhb.at[2, 0], dh=1)
    zh_m[1].wait_recv()
    f_m = send(zhb.at[1, 1], zhb.at[2, 1], dh=3)

    def want(tile, r):
        return tile[r : r + 1, :]

    def pick(buf, index, n, first):
        out = buf(0)
        for d in range(1, n):
            out = jnp.where(index == (first + d) % n, buf(d), out)
        return out

    def near_hit(kk, i):
        dx, dc = NEAR[i]
        return (kk // (NL * NC) == (x + dx) % NX) & (kk % NC == (c + dc) % NC)

    for cp in ask + near:
        cp.wait_recv()
    along_l = []
    for d in range(NL):
        kk = want(reql[d], 0)
        a = nb[0]
        for i in range(1, len(NEAR)):
            a = jnp.where(near_hit(kk, i), nb[i], a)
        if d:
            lsel[d] = a
            along_l.append(send(lsel.at[d], lrecv.at[NL - d], dl=d))
        else:
            lrecv[0] = a

    along_y = [[], []]
    for half, cps in enumerate(((zh_m[0], f_p), (zh_p[1], f_m))):
        for cp in cps:
            cp.wait_recv()
        for d in range(NY):
            mm = want(reqy[d], 1)
            b = pick(lambda e: zhb[e, half], mm % NH, NH, h)
            if d:
                bsend[d, half] = b
                along_y[half].append(send(bsend.at[d, half], brecv.at[NY - d, half], dy=d))
            else:
                brecv[0, half] = b

    for cp in along_l:
        cp.wait_recv()
    aop[...] = pick(lambda e: lrecv[e], (want(req[...], 0) // NC) % NL, NL, l)
    item = jnp.concatenate([unpack(aop, 0), unpack(aop, 1)], axis=1)
    centre = jnp.mean(item[0:3], axis=1, keepdims=True)
    ax, aal, ahs = item[0:3] - centre, item[3:6], 0.5 * item[6:7] * item[6:7]
    left[...] = metric(ax, ahs)[0]
    ea[...], fa[...] = moments(ax, aal)
    col[...] = column(1.5 * ahs)

    def column_half(half):
        for cp in along_y[half]:
            cp.wait_recv()
        bop[half] = pick(lambda e: brecv[e, half], want(req[...], 1) // NH, NY, y)
        item = unpack(bop, half)
        bx, bal, bhs = item[0:3] - centre, item[3:6], 0.5 * item[6:7] * item[6:7]
        js = pl.ds(512 * half, 512)
        right[:, js] = metric(bx, bhs)[1]
        eb[:, js], fb[:, js] = moments(bx, bal)
        rowj[:, js] = 1.5 * bhs
        return bx, bal

    back_y, sums = [None] * NB, [None] * NB

    def give_back(q):
        bx, bal = cols[q // 2]
        js = slice((q % 2) * TJ, (q % 2) * TJ + TJ)
        pack(pb, q, finish(bx[:, js], bal[:, js], *sums[q]), 0, 2)
        back_y[q] = [send(pb.at[q], yrecv.at[NY - d, q], dy=d) for d in (1, 2, 3)]
        yrecv[0, q] = pb[q]

    cols = [column_half(0)]
    sums[0] = block(0, True)
    sums[1] = block(1, True)
    cols.append(column_half(1))
    give_back(0)
    sums[2] = block(2, True)
    give_back(1)
    sums[3] = block(3, True)
    give_back(2)
    give_back(3)
    back_l = []
    rows = finish(ax, aal, sga[...], sha[...])
    for half in range(2):
        pack(pa, half, rows[:, 512 * half : 512 * half + 512], 0, 4)
        back_l.append([send(pa.at[half], lback.at[NL - d, half], dl=d) for d in (1, 2, 3)])
        lback[0, half] = pa[half]

    masks = []
    for d in range(NY):
        t = reqy[d]
        kk, mm, on = want(t, 0), want(t, 1), want(t, 2)
        self_pair = (mm == ((y + d) % NY) * NH + h) & (kk == (x * NL + l) * NC + c)
        mine = (on == 1) & (mm // NH == y) & jnp.logical_not(self_pair)
        masks.append([mine & (mm % NH == (h + e) % NH) for e in range(NH)])
    back_h = []
    for q in range(NB):
        for cp in back_y[q]:
            cp.wait_recv()
        for e in (2, 1, 3, 0):
            total = jnp.zeros((12, 128), f32)
            for d in range(NY):
                total = total + jnp.where(masks[d][e], yrecv[d, q], 0.0)
            if e:
                hsend[e, q] = total
                back_h.append(send(hsend.at[e, q], hrecv.at[NH - e, q], dh=e))
            else:
                hrecv[0, q] = total

    masks = []
    for d in range(NL):
        t = reql[d]
        kk, on = want(t, 0), want(t, 2)
        mine = (on == 1) & ((kk // NC) % NL == l)
        masks.append([mine & near_hit(kk, i) for i in range(len(NEAR))])
    back_n = []
    for half in range(2):
        for cp in back_l[half]:
            cp.wait_recv()
        for i in list(range(1, len(NEAR))) + [0]:
            total = jnp.zeros((24, 128), f32)
            for d in range(NL):
                total = total + jnp.where(masks[d][i], lback[d, half], 0.0)
            if i:
                nsend[i, half] = total
                dx, dc = NEAR[i]
                back_n.append(send(nsend.at[i, half], nrecv.at[near_slot(dx, dc), half], dx=dx, dc=dc))
            else:
                nrecv[0, half] = total

    for cp in sent:
        cp.wait_send()
    for cp in back_n:
        cp.wait_recv()
    for half in range(2):
        total = nrecv[0, half]
        for i in range(1, len(NEAR)):
            total = total + nrecv[i, half]
        pa[half] = total
    for cp in back_h:
        cp.wait_recv()
    for q in range(NB):
        pb[q] = (hrecv[0, q] + hrecv[1, q]) + (hrecv[2, q] + hrecv[3, q])
    for t in range(8):
        lanes = slice(128 * t, 128 * t + 128)
        out = (sout[:, lanes] + pa[t // 4, pl.ds(t % 4, 6, stride=4), :]
               + pb[t // 2, pl.ds(t % 2, 6, stride=2), :])
        result[:, lanes] = out
    assert used[0] == N_COPIES


N_COPIES = 4 + 7 + 6 + 2 + 3 + 6 + 12 + 6 + 12 + 14


def local(positions, strengths, radii, pair_list, pair_count):
    vm, sm = pl.BlockSpec(memory_space=pltpu.VMEM), pl.BlockSpec(memory_space=pltpu.SMEM)
    hbm = pl.BlockSpec(memory_space=pltpu.HBM)
    V = pltpu.VMEM
    out = jax.ShapeDtypeStruct((6, G), f32)
    item = (2, 28, 128)
    result = pl.pallas_call(
        kernel,
        out_shape=out,
        in_specs=[hbm, hbm, hbm, sm, sm],
        out_specs=vm,
        scratch_shapes=[
            V((3, G), f32), V((3, G), f32), V((8, 128), f32),
            V(item, f32), V((8, 128), jnp.int32), V((NH,) + item, f32),
            V((NY, 8, 128), jnp.int32), V((NL, 8, 128), jnp.int32),
            V((8,) + item, f32), V((NL,) + item, f32), V((NL,) + item, f32),
            V((NY,) + item, f32), V((NY,) + item, f32), V(item, f32), V(item, f32),
            V((NB, 12, 128), f32), V((NY, NB, 12, 128), f32), V((NH, NB, 12, 128), f32), V((NH, NB, 12, 128), f32),
            V((2, 24, 128), f32), V((NL, 2, 24, 128), f32), V((8, 2, 24, 128), f32), V((8, 2, 24, 128), f32),
            V((48, G), bf16), V((48, G), bf16), V((G, 128), f32), V((1, G), f32),
            V((24, G), bf16), V((96, G), bf16), V((24, G), bf16), V((96, G), bf16),
            V((8, G), f32), V((32, G), f32), V((6, G), f32),
            pltpu.SemaphoreType.DMA((3,)), pltpu.SemaphoreType.DMA((N_COPIES,)), pltpu.SemaphoreType.DMA((N_COPIES,)),
        ],
        compiler_params=pltpu.CompilerParams(
            collective_id=0, has_side_effects=True, vmem_limit_bytes=64 * 2**20 - 2**16
        ),
        cost_estimate=pl.CostEstimate(flops=2 * G * G * 256, bytes_accessed=64 * G, transcendentals=2 * G * G),
        name="vortex_pairs",
    )(positions, strengths, radii.reshape(8, 128), pair_list, pair_count)
    return result[:3], result[3:]


def solution(mesh):
    placed = (
        P(None, ("row", "col")),
        P(None, ("row", "col")),
        P(("row", "col")),
        P(None, "row", "col", None),
        P("row", "col"),
    )
    return jax.shard_map(
        local,
        mesh=mesh,
        in_specs=placed,
        out_specs=(P(None, ("row", "col")), P(None, ("row", "col"))),
        check_vma=False,
    )
```

```python
import functools
import math

import jax
import jax.numpy as jnp
from jax import lax
from jax.experimental import pallas as pl
from jax.experimental.pallas import tpu as pltpu
from jax.sharding import PartitionSpec as P

G = 1024
MESH = pl.DeviceIdType.MESH
f32, bf16 = jnp.float32, jnp.bfloat16
TJ = 256
NB = G // TJ

NY, NH, NX, NL, NC = 4, 4, 4, 4, 2
NEAR = [(dx, dc) for dx in range(NX) for dc in range(NC)]


def coords():
    r, c = lax.axis_index("row"), lax.axis_index("col")
    return r // NH, r % NH, c // (NL * NC), (c // NC) % NL, c % NC


def at(dy=0, dh=0, dx=0, dl=0, dc=0):
    y, h, x, l, c = coords()
    row = ((y + dy) % NY) * NH + (h + dh) % NH
    col = (((x + dx) % NX) * NL + (l + dl) % NL) * NC + (c + dc) % NC
    return {"row": row, "col": col}


def split3(v):
    h = v.astype(bf16).astype(f32)
    rest = v - h
    m = rest.astype(bf16).astype(f32)
    return h, m, rest - m


def cross(p, q):
    return [p[1] * q[2] - p[2] * q[1], p[2] * q[0] - p[0] * q[2], p[0] * q[1] - p[1] * q[0]]


def rows_of(v, n):
    return [v[i : i + 1] for i in range(n)]


def unpack(ref, q):
    return jnp.concatenate([ref[q, pl.ds(s, 7, stride=2), :] for s in range(2)], axis=1)


def unpack_all(ref):
    return jnp.concatenate([unpack(ref, q) for q in range(NB)], axis=1)


def pack(ref, q, v, first):
    for s in range(2):
        ref[q, pl.ds(2 * first + s, v.shape[0], stride=2), :] = v[:, s * 128 : (s + 1) * 128]


def metric(x, hs):
    n = x.shape[1]
    u = x[0:1] * x[0:1] + x[1:2] * x[1:2] + x[2:3] * x[2:3] + hs
    one, zero = jnp.ones((1, n), f32), jnp.zeros((3, n), f32)
    lh, lm, ll = split3(jnp.concatenate([-2.0 * x, u, one, zero], 0))
    rh, rm, rl = split3(jnp.concatenate([x, one, u, zero], 0))
    left = jnp.concatenate([lh, lh, lm, lm, lh, ll], 0).astype(bf16)
    right = jnp.concatenate([rh, rm, rh, rm, rl, rh], 0).astype(bf16)
    return left, right


def moments(x, al):
    e = jnp.concatenate([al] + cross(rows_of(x, 3), rows_of(al, 3)) + [jnp.zeros((2, x.shape[1]), f32)], 0)
    f = jnp.concatenate([e, x[0:1] * e, x[1:2] * e, x[2:3] * e], 0)
    return jnp.concatenate(split3(e), 0).astype(bf16), jnp.concatenate(split3(f), 0).astype(bf16)


def finish(x, al, sg, sh):
    xs, a = rows_of(x, 3), rows_of(al, 3)
    g0, g1 = rows_of(sg[0:3], 3), rows_of(sg[3:6], 3)
    sh = -5.0 * sh
    row = lambda p, q: sh[8 * p + q : 8 * p + q + 1]
    h0, h1 = [row(0, q) for q in range(3)], [row(0, 3 + q) for q in range(3)]
    at0 = [a[0] * row(1, q) + a[1] * row(2, q) + a[2] * row(3, q) for q in range(3)]
    at1 = [a[0] * row(1, 3 + q) + a[1] * row(2, 3 + q) + a[2] * row(3, 3 + q) for q in range(3)]
    ax = a[0] * xs[0] + a[1] * xs[1] + a[2] * xs[2]
    c0, c1, c2, c3 = cross(xs, g0), cross(xs, h0), cross(xs, at0), cross(a, g0)
    scale = 1.0 / (4.0 * math.pi)
    vel = [scale * (g1[i] - c0[i]) for i in range(3)]
    stretch = [-scale * (c3[i] + ax * (c1[i] - h1[i]) - c2[i] + at1[i]) for i in range(3)]
    return jnp.concatenate(vel + stretch, 0)


def dot(a, b, dims):
    return lax.dot_general(a, b, (dims, ((), ())), preferred_element_type=f32)


def halves(v):
    h = v.astype(bf16)
    return h, (v - h.astype(f32)).astype(bf16)


def kernels_of(left, right, si, sj):
    y = lax.rsqrt(dot(left, right, ((0,), (0,))))
    y2 = y * y
    p = y2 * y
    t = (si + sj) * y2
    return halves(p + p * t) + halves((p * y2) * (0.6 + t))


def fold(hi, lo, n):
    return (hi[:n] + hi[n : 2 * n] + hi[2 * n :]) + (lo[:n] + lo[n:])


def column(hs):
    return jnp.transpose(jnp.broadcast_to(hs, (128, hs.shape[1])))


def kernel(pos_in, stg_in, rad_in, plist, pcount, result,
           pos, stg, rad, own, req, zhb, reqy, reql, reqn, nb, lsel, lrecv, bsend, brecv, aop, bop,
           pb, yrecv, hsend, hrecv, pa, nrecv, lsend, lback,
           left, right, col, rowj, ea, fa, eb, fb, kept, sout, lsem, ssem, rsem):
    y, h, x, l, c = coords()
    bar = pltpu.get_barrier_semaphore()
    peers = (
        [dict(dh=1), dict(dh=3)]
        + [dict(dx=dx, dc=dc) for dx, dc in NEAR[1:]]
        + [dict(dl=d) for d in (1, 2, 3)]
        + [dict(dy=d) for d in (1, 2, 3)]
    )
    @pl.when(h == 0)
    def _():
        pl.semaphore_signal(bar, inc=1, device_id=at(dh=2), device_id_type=MESH)

    for o in peers:
        pl.semaphore_signal(bar, inc=1, device_id=at(**o), device_id_type=MESH)
    loads = [
        pltpu.make_async_copy(src, dst, lsem.at[i])
        for i, (src, dst) in enumerate([(pos_in, pos), (stg_in, stg), (rad_in, rad)])
    ]
    for cp in loads:
        cp.start()

    used = [0]
    sent = []

    def slot():
        used[0] += 1
        return used[0] - 1

    def prep(src, dst, i, r, **o):
        return pltpu.make_async_remote_copy(
            src_ref=src, dst_ref=dst, send_sem=ssem.at[i], recv_sem=rsem.at[r],
            device_id=at(**o), device_id_type=MESH)

    def send(src, dst, **o):
        i = slot()
        cp = prep(src, dst, i, i, **o)
        cp.start()
        sent.append(cp)
        return cp

    k, m, live = plist[0, 0, 0, 1], plist[1, 0, 0, 1], (pcount[0, 0] > 1).astype(jnp.int32)
    ri = lax.broadcasted_iota(jnp.int32, (8, 128), 0)
    req[...] = jnp.where(ri == 0, k, jnp.where(ri == 1, m, live))
    for cp in loads:
        cp.wait()
    for q in range(NB):
        js = slice(TJ * q, TJ * q + TJ)
        pack(own, q, pos[:, js], 0)
        pack(own, q, stg[:, js], 3)
        own[q, 12:14, :] = rad[2 * q : 2 * q + 2, :]

    item = unpack_all(own)
    own_x, own_al, own_r = item[0:3], item[3:6], item[6:7]
    own_x = own_x - jnp.mean(own_x, axis=1, keepdims=True)
    own_hs = 0.5 * own_r * own_r
    left[...], right[...] = metric(own_x, own_hs)
    ea[...], fa[...] = moments(own_x, own_al)
    rowj[...] = 1.5 * own_hs
    col[...] = column(1.5 * own_hs)

    def block(q, keep):
        js = pl.ds(q * TJ, TJ)
        si = jnp.concatenate([col[...]] * (TJ // 128), 1)
        parts = kernels_of(left[...], right[:, js], si, rowj[:, js])
        gh, gl, hh, hl = parts
        if keep:
            for i in range(4):
                kept[i, :, js] = parts[i]
        d = ((1,), (0,))
        sg = fold(dot(ea[...], gh, d), dot(ea[:16], gl, d), 8)
        sh = fold(dot(fa[...], hh, d), dot(fa[:64], hl, d), 32)
        return sg, sh

    def row_block(p):
        rs = pl.ds(p * TJ, TJ)
        d = ((1,), (1,))
        sg = fold(dot(eb[...], kept[0, rs, :], d), dot(eb[:16], kept[1, rs, :], d), 8)
        sh = fold(dot(fb[...], kept[2, rs, :], d), dot(fb[:64], kept[3, rs, :], d), 32)
        return sg, sh

    def own_block(q):
        js = slice(q * TJ, q * TJ + TJ)
        sout[:, js] = finish(own_x[:, js], own_al[:, js], *block(q, False))

    pl.semaphore_wait(bar, len(peers) + (h // 2) * (1 - h % 2))
    ways = ((1, 0), (3, 2), (1, 1), (3, 3))
    ahead, across = {}, {}
    for d, q in ways:
        i = slot()
        ahead[q] = prep(zhb.at[NH - d, pl.ds(q, 1)], zhb.at[2, pl.ds(q, 1)], i, i, dh=d)
        across[q] = prep(own.at[pl.ds(q, 1)], zhb.at[2, pl.ds(q, 1)], slot(), i, dh=2)

    @pl.when(h == 2)
    def _():
        for d, q in ways:
            across[q].start()

    def to_zh(q, n, d):
        return send(own.at[pl.ds(q, n)], zhb.at[NH - d, pl.ds(q, n)], dh=d)

    first = {(d, q): to_zh(q, 1, d) for d, q in ways}
    rest = {1: to_zh(2, 2, 1), 3: to_zh(0, 2, 3)}

    def near_slot(dx, dc):
        return ((NX - dx) % NX) * NC + dc

    ask_y = [send(req, reqy.at[NY - d], dy=d) for d in (1, 2, 3)]
    ask_l = [send(req, reql.at[NL - d], dl=d) for d in (1, 2, 3)]
    near = [
        [send(own.at[pl.ds(q, 2)], nb.at[near_slot(dx, dc), pl.ds(q, 2)], dx=dx, dc=dc) for dx, dc in NEAR[1:]]
        for q in (0, 2)
    ]
    ask_n = [send(req, reqn.at[near_slot(dx, dc)], dx=dx, dc=dc) for dx, dc in NEAR[1:]]
    zhb[0] = own[...]
    nb[0] = own[...]
    reql[0] = req[...]
    reqy[0] = req[...]
    reqn[0] = req[...]
    for q in range(NB):
        own_block(q)

    for d, q in ways:
        first[d, q].wait_recv()

        @pl.when(h != NH - d)
        def _():
            ahead[q].start()

    def want(tile, r):
        return tile[r : r + 1, :]

    def pick(buf, index, n, first):
        out = buf(0)
        for d in range(1, n):
            out = jnp.where(index == (first + d) % n, buf(d), out)
        return out

    def near_hit(kk, i):
        dx, dc = NEAR[i]
        return (kk // (NL * NC) == (x + dx) % NX) & (kk % NC == (c + dc) % NC)

    for cp in ask_l:
        cp.wait_recv()
    along_l = []
    for half in range(2):
        for cp in near[half]:
            cp.wait_recv()
        qs = pl.ds(2 * half, 2)
        for d in (1, 2, 3, 0):
            kk = want(reql[d], 0)
            a = nb[0, qs]
            for i in range(1, len(NEAR)):
                a = jnp.where(near_hit(kk, i), nb[i, qs], a)
            if d:
                lsel[d, qs] = a
                along_l.append(send(lsel.at[d, qs], lrecv.at[NL - d, qs], dl=d))
            else:
                lrecv[0, qs] = a

    for cp in ask_y + list(rest.values()):
        cp.wait_recv()
    order = (0, 2, 1, 3)
    along_y = {}
    for q in order:
        ahead[q].wait_recv()
        along_y[q] = []
        for d in (2, 1, 3, 0):
            b = pick(lambda e: zhb[e, q], want(reqy[d], 1) % NH, NH, h)
            if d:
                bsend[d, q] = b
                along_y[q].append(send(bsend.at[d, q], brecv.at[NY - d, q], dy=d))
            else:
                brecv[0, q] = b

    for cp in along_l:
        cp.wait_recv()
    aop[...] = pick(lambda e: lrecv[e], (want(req[...], 0) // NC) % NL, NL, l)
    item = unpack_all(aop)
    centre = jnp.mean(item[0:3], axis=1, keepdims=True)
    ax, aal, ahs = item[0:3] - centre, item[3:6], 0.5 * item[6:7] * item[6:7]
    left[...] = metric(ax, ahs)[0]
    ea[...], fa[...] = moments(ax, aal)
    col[...] = column(1.5 * ahs)

    back_y = {}
    for q in order:
        for cp in along_y[q]:
            cp.wait_recv()
        bop[q] = pick(lambda e: brecv[e, q], want(req[...], 1) // NH, NY, y)
        item = unpack(bop, q)
        bx, bal, bhs = item[0:3] - centre, item[3:6], 0.5 * item[6:7] * item[6:7]
        js = pl.ds(q * TJ, TJ)
        right[:, js] = metric(bx, bhs)[1]
        eb[:, js], fb[:, js] = moments(bx, bal)
        rowj[:, js] = 1.5 * bhs
        pack(pb, q, finish(bx, bal, *block(q, True)), 0)
        back_y[q] = [send(pb.at[q], yrecv.at[NY - d, q], dy=d) for d in (2, 1, 3)]
        yrecv[0, q] = pb[q]

    masks_h = []
    for d in range(NY):
        t = reqy[d]
        kk, mm, on = want(t, 0), want(t, 1), want(t, 2)
        self_pair = (mm == ((y + d) % NY) * NH + h) & (kk == (x * NL + l) * NC + c)
        mine = (on == 1) & (mm // NH == y) & jnp.logical_not(self_pair)
        masks_h.append([mine & (mm % NH == (h + e) % NH) for e in range(NH)])
    back_h = []

    def to_owner_h(q, es):
        for e in es:
            total = jnp.zeros((12, 128), f32)
            for d in range(NY):
                total = total + jnp.where(masks_h[d][e], yrecv[d, q], 0.0)
            if e:
                hsend[e, q] = total
                back_h.append(send(hsend.at[e, q], hrecv.at[NH - e, q], dh=e))
            else:
                hrecv[0, q] = total

    back_n = []
    for p, q in enumerate(order):
        rs = slice(p * TJ, p * TJ + TJ)
        pack(pa, p, finish(ax[:, rs], aal[:, rs], *row_block(p)), 0)
        back_n.append([send(pa.at[p], nrecv.at[near_slot(dx, dc), p], dx=dx, dc=dc) for dx, dc in NEAR[1:]])
        nrecv[0, p] = pa[p]
        for cp in back_y[q]:
            cp.wait_recv()
        to_owner_h(q, (2,))
        if p:
            to_owner_h(order[p - 1], (1, 3))
    to_owner_h(order[3], (1, 3))

    for cp in ask_n:
        cp.wait_recv()
    masks_l = []
    for i in range(len(NEAR)):
        t = reqn[i]
        kk, on = want(t, 0), want(t, 2)
        mine = (on == 1) & (kk // (NL * NC) == x) & (kk % NC == c)
        masks_l.append([mine & ((kk // NC) % NL == (l + e) % NL) for e in range(NL)])
    back_l = []
    for p in range(NB):
        for cp in back_n[p]:
            cp.wait_recv()
        for e in (3, 2, 1, 0):
            total = jnp.zeros((12, 128), f32)
            for i in range(len(NEAR)):
                total = total + jnp.where(masks_l[i][e], nrecv[i, p], 0.0)
            if e:
                lsend[e, p] = total
                back_l.append(send(lsend.at[e, p], lback.at[NL - e, p], dl=e))
            else:
                lback[0, p] = total

    for q in range(NB):
        to_owner_h(q, (0,))
    for cp in sent:
        cp.wait_send()

    @pl.when(h == 2)
    def _():
        for cp in across.values():
            cp.wait_send()

    for d in (1, 3):
        @pl.when(h != NH - d)
        def _():
            for e, q in ways:
                if e == d:
                    ahead[q].wait_send()

    for cp in back_l + back_h:
        cp.wait_recv()
    for q in range(NB):
        pb[q] = ((hrecv[0, q] + hrecv[1, q]) + (hrecv[2, q] + hrecv[3, q])) + (
            (lback[0, q] + lback[1, q]) + (lback[2, q] + lback[3, q]))
    for t in range(8):
        lanes = slice(128 * t, 128 * t + 128)
        result[:, lanes] = sout[:, lanes] + pb[t // 2, pl.ds(t % 2, 6, stride=2), :]
    assert used[0] == N_COPIES


N_COPIES = 6 + 3 + 3 + 14 + 7 + 8 + 6 + 12 + 12 + 28 + 12 + 12


def local(positions, strengths, radii, pair_list, pair_count):
    vm, sm = pl.BlockSpec(memory_space=pltpu.VMEM), pl.BlockSpec(memory_space=pltpu.SMEM)
    hbm = pl.BlockSpec(memory_space=pltpu.HBM)
    V = pltpu.VMEM
    out = jax.ShapeDtypeStruct((6, G), f32)
    item, part = (NB, 14, 128), (NB, 12, 128)
    ask = (8, 128)
    result = pl.pallas_call(
        kernel,
        out_shape=out,
        in_specs=[hbm, hbm, hbm, sm, sm],
        out_specs=vm,
        scratch_shapes=[
            V((3, G), f32), V((3, G), f32), V((8, 128), f32),
            V(item, f32), V(ask, jnp.int32), V((NH,) + item, f32),
            V((NY,) + ask, jnp.int32), V((NL,) + ask, jnp.int32), V((8,) + ask, jnp.int32),
            V((8,) + item, f32), V((NL,) + item, f32), V((NL,) + item, f32),
            V((NY,) + item, f32), V((NY,) + item, f32), V(item, f32), V(item, f32),
            V(part, f32), V((NY,) + part, f32), V((NH,) + part, f32), V((NH,) + part, f32),
            V(part, f32), V((8,) + part, f32), V((NL,) + part, f32), V((NL,) + part, f32),
            V((48, G), bf16), V((48, G), bf16), V((G, 128), f32), V((1, G), f32),
            V((24, G), bf16), V((96, G), bf16), V((24, G), bf16), V((96, G), bf16),
            V((4, G, G), bf16), V((6, G), f32),
            pltpu.SemaphoreType.DMA((3,)), pltpu.SemaphoreType.DMA((N_COPIES,)), pltpu.SemaphoreType.DMA((N_COPIES,)),
        ],
        compiler_params=pltpu.CompilerParams(
            collective_id=0, has_side_effects=True, vmem_limit_bytes=64 * 2**20 - 2**16
        ),
        cost_estimate=pl.CostEstimate(flops=2 * G * G * 256, bytes_accessed=64 * G, transcendentals=2 * G * G),
        name="vortex_pairs",
    )(positions, strengths, radii.reshape(8, 128), pair_list, pair_count)
    return result[:3], result[3:]


def solution(mesh):
    placed = (
        P(None, ("row", "col")),
        P(None, ("row", "col")),
        P(("row", "col")),
        P(None, "row", "col", None),
        P("row", "col"),
    )
    return jax.shard_map(
        local,
        mesh=mesh,
        in_specs=placed,
        out_specs=(P(None, ("row", "col")), P(None, ("row", "col"))),
        check_vma=False,
    )
```

```python
import functools
import math

import jax
import jax.numpy as jnp
from jax import lax
from jax.experimental import pallas as pl
from jax.experimental.pallas import tpu as pltpu
from jax.sharding import PartitionSpec as P

G = 1024
MESH = pl.DeviceIdType.MESH
f32, bf16 = jnp.float32, jnp.bfloat16
TJ = 256
NB = G // TJ

NY, NH, NX, NL, NC = 4, 4, 4, 4, 2
NEAR = [(dx, dc) for dx in range(NX) for dc in range(NC)]


def coords():
    r, c = lax.axis_index("row"), lax.axis_index("col")
    return r // NH, r % NH, c // (NL * NC), (c // NC) % NL, c % NC


def at(dy=0, dh=0, dx=0, dl=0, dc=0):
    y, h, x, l, c = coords()
    row = ((y + dy) % NY) * NH + (h + dh) % NH
    col = (((x + dx) % NX) * NL + (l + dl) % NL) * NC + (c + dc) % NC
    return {"row": row, "col": col}


def split3(v):
    h = v.astype(bf16).astype(f32)
    rest = v - h
    m = rest.astype(bf16).astype(f32)
    return h, m, rest - m


def cross(p, q):
    return [p[1] * q[2] - p[2] * q[1], p[2] * q[0] - p[0] * q[2], p[0] * q[1] - p[1] * q[0]]


def rows_of(v, n):
    return [v[i : i + 1] for i in range(n)]


def unpack(ref, q):
    return jnp.concatenate([ref[q, pl.ds(s, 7, stride=2), :] for s in range(2)], axis=1)


def unpack_all(ref):
    return jnp.concatenate([unpack(ref, q) for q in range(NB)], axis=1)


def pack(ref, q, v):
    for s in range(2):
        ref[q, pl.ds(s, 6, stride=2), :] = v[:, s * 128 : (s + 1) * 128]


def metric(x, hs):
    n = x.shape[1]
    u = x[0:1] * x[0:1] + x[1:2] * x[1:2] + x[2:3] * x[2:3] + hs
    one, zero = jnp.ones((1, n), f32), jnp.zeros((3, n), f32)
    lh, lm, ll = split3(jnp.concatenate([-2.0 * x, u, one, zero], 0))
    rh, rm, rl = split3(jnp.concatenate([x, one, u, zero], 0))
    left = jnp.concatenate([lh, lh, lm, lm, lh, ll], 0).astype(bf16)
    right = jnp.concatenate([rh, rm, rh, rm, rl, rh], 0).astype(bf16)
    return left, right


def moments(x, al):
    e = jnp.concatenate([al] + cross(rows_of(x, 3), rows_of(al, 3)) + [jnp.zeros((2, x.shape[1]), f32)], 0)
    f = jnp.concatenate([e, x[0:1] * e, x[1:2] * e, x[2:3] * e], 0)
    return jnp.concatenate(split3(e), 0).astype(bf16), jnp.concatenate(split3(f), 0).astype(bf16)


def finish(x, al, sg, sh):
    xs, a = rows_of(x, 3), rows_of(al, 3)
    g0, g1 = rows_of(sg[0:3], 3), rows_of(sg[3:6], 3)
    sh = -5.0 * sh
    row = lambda p, q: sh[8 * p + q : 8 * p + q + 1]
    h0, h1 = [row(0, q) for q in range(3)], [row(0, 3 + q) for q in range(3)]
    at0 = [a[0] * row(1, q) + a[1] * row(2, q) + a[2] * row(3, q) for q in range(3)]
    at1 = [a[0] * row(1, 3 + q) + a[1] * row(2, 3 + q) + a[2] * row(3, 3 + q) for q in range(3)]
    ax = a[0] * xs[0] + a[1] * xs[1] + a[2] * xs[2]
    c0, c1, c2, c3 = cross(xs, g0), cross(xs, h0), cross(xs, at0), cross(a, g0)
    scale = 1.0 / (4.0 * math.pi)
    vel = [scale * (g1[i] - c0[i]) for i in range(3)]
    stretch = [-scale * (c3[i] + ax * (c1[i] - h1[i]) - c2[i] + at1[i]) for i in range(3)]
    return jnp.concatenate(vel + stretch, 0)


def dot(a, b, dims):
    return lax.dot_general(a, b, (dims, ((), ())), preferred_element_type=f32)


def halves(v):
    h = v.astype(bf16)
    return h, (v - h.astype(f32)).astype(bf16)


def kernels_of(left, right, si, sj):
    y = lax.rsqrt(dot(left, right, ((0,), (0,))))
    y2 = y * y
    p = y2 * y
    t = (si + sj) * y2
    return halves(p + p * t) + halves((p * y2) * (0.6 + t))


def fold(hi, lo, n):
    return (hi[:n] + hi[n : 2 * n] + hi[2 * n :]) + (lo[:n] + lo[n:])


def column(hs):
    return jnp.transpose(jnp.broadcast_to(hs, (128, hs.shape[1])))


def kernel(pos_in, stg_in, rad_in, plist, pcount, result,
           pos, stg, rad, own, req, zhb, reqy, reql, reqn, nb, lsel, lrecv, bsend, brecv, aop, bop,
           pb, yrecv, hsend, hrecv, pa, nrecv, lsend, lback,
           left, right, col, rowj, ea, fa, eb, fb, kept, sout, lsem, ssem, rsem):
    y, h, x, l, c = coords()
    bar = pltpu.get_barrier_semaphore()
    peers = (
        [dict(dh=1), dict(dh=3)]
        + [dict(dx=dx, dc=dc) for dx, dc in NEAR[1:]]
        + [dict(dl=d) for d in (1, 2, 3)]
        + [dict(dy=d) for d in (1, 2, 3)]
    )
    @pl.when(h == 0)
    def _():
        pl.semaphore_signal(bar, inc=1, device_id=at(dh=2), device_id_type=MESH)

    for o in peers:
        pl.semaphore_signal(bar, inc=1, device_id=at(**o), device_id_type=MESH)
    loads = [
        pltpu.make_async_copy(src, dst, lsem.at[i])
        for i, (src, dst) in enumerate([(pos_in, pos), (stg_in, stg), (rad_in, rad)])
    ]
    for cp in loads:
        cp.start()

    used = [0]
    sent = []

    def slot():
        used[0] += 1
        return used[0] - 1

    def prep(src, dst, i, r, **o):
        return pltpu.make_async_remote_copy(
            src_ref=src, dst_ref=dst, send_sem=ssem.at[i], recv_sem=rsem.at[r],
            device_id=at(**o), device_id_type=MESH)

    def send(src, dst, **o):
        i = slot()
        cp = prep(src, dst, i, i, **o)
        cp.start()
        sent.append(cp)
        return cp

    k, m, live = plist[0, 0, 0, 1], plist[1, 0, 0, 1], (pcount[0, 0] > 1).astype(jnp.int32)
    ri = lax.broadcasted_iota(jnp.int32, (8, 128), 0)
    req[...] = jnp.where(ri == 0, k, jnp.where(ri == 1, m, live))
    for cp in loads:
        cp.wait()
    for q in range(NB):
        js = slice(TJ * q, TJ * q + TJ)
        pack(own, q, jnp.concatenate([pos[:, js], stg[:, js]], axis=0))
        own[q, 12:14, :] = rad[2 * q : 2 * q + 2, :]

    item = unpack_all(own)
    own_x, own_al, own_r = item[0:3], item[3:6], item[6:7]
    own_x = own_x - jnp.mean(own_x, axis=1, keepdims=True)
    own_hs = 0.5 * own_r * own_r
    left[...], right[...] = metric(own_x, own_hs)
    ea[...], fa[...] = moments(own_x, own_al)
    rowj[...] = 1.5 * own_hs
    col[...] = column(1.5 * own_hs)

    def block(q, keep):
        js = pl.ds(q * TJ, TJ)
        si = jnp.concatenate([col[...]] * (TJ // 128), 1)
        parts = kernels_of(left[...], right[:, js], si, rowj[:, js])
        gh, gl, hh, hl = parts
        if keep:
            for i in range(4):
                kept[i, :, js] = parts[i]
        d = ((1,), (0,))
        sg = fold(dot(ea[...], gh, d), dot(ea[:16], gl, d), 8)
        sh = fold(dot(fa[...], hh, d), dot(fa[:64], hl, d), 32)
        return sg, sh

    def row_block(p):
        rs = pl.ds(p * TJ, TJ)
        d = ((1,), (1,))
        sg = fold(dot(eb[...], kept[0, rs, :], d), dot(eb[:16], kept[1, rs, :], d), 8)
        sh = fold(dot(fb[...], kept[2, rs, :], d), dot(fb[:64], kept[3, rs, :], d), 32)
        return sg, sh

    def own_block(q):
        js = slice(q * TJ, q * TJ + TJ)
        sout[:, js] = finish(own_x[:, js], own_al[:, js], *block(q, False))

    pl.semaphore_wait(bar, len(peers) + (h // 2) * (1 - h % 2))
    ways = ((1, 0), (3, 2), (1, 1), (3, 3))
    ahead, across = {}, {}
    for d, q in ways:
        i = slot()
        ahead[q] = prep(zhb.at[NH - d, pl.ds(q, 1)], zhb.at[2, pl.ds(q, 1)], i, i, dh=d)
        across[q] = prep(own.at[pl.ds(q, 1)], zhb.at[2, pl.ds(q, 1)], slot(), i, dh=2)

    @pl.when(h == 2)
    def _():
        for d, q in ways:
            across[q].start()

    def to_zh(q, n, d):
        return send(own.at[pl.ds(q, n)], zhb.at[NH - d, pl.ds(q, n)], dh=d)

    first = {(d, q): to_zh(q, 1, d) for d, q in ways}
    rest = {1: to_zh(2, 2, 1), 3: to_zh(0, 2, 3)}

    def near_slot(dx, dc):
        return ((NX - dx) % NX) * NC + dc

    ask_y = [send(req, reqy.at[NY - d], dy=d) for d in (1, 2, 3)]
    ask_l = [send(req, reql.at[NL - d], dl=d) for d in (1, 2, 3)]
    near = [
        [send(own.at[pl.ds(q, 2)], nb.at[near_slot(dx, dc), pl.ds(q, 2)], dx=dx, dc=dc) for dx, dc in NEAR[1:]]
        for q in (0, 2)
    ]
    ask_n = [send(req, reqn.at[near_slot(dx, dc)], dx=dx, dc=dc) for dx, dc in NEAR[1:]]
    zhb[0] = own[...]
    nb[0] = own[...]
    reql[0] = req[...]
    reqy[0] = req[...]
    reqn[0] = req[...]
    for q in range(NB):
        own_block(q)

    for d, q in ways:
        first[d, q].wait_recv()

        @pl.when(h != NH - d)
        def _():
            ahead[q].start()

    def want(tile, r):
        return tile[r : r + 1, :]

    def pick(buf, index, n, first):
        out = buf(0)
        for d in range(1, n):
            out = jnp.where(index == (first + d) % n, buf(d), out)
        return out

    def near_hit(kk, i):
        dx, dc = NEAR[i]
        return (kk // (NL * NC) == (x + dx) % NX) & (kk % NC == (c + dc) % NC)

    for cp in ask_l:
        cp.wait_recv()
    along_l = []
    for half in range(2):
        for cp in near[half]:
            cp.wait_recv()
        qs = pl.ds(2 * half, 2)
        for d in (1, 2, 3, 0):
            kk = want(reql[d], 0)
            a = nb[0, qs]
            for i in range(1, len(NEAR)):
                a = jnp.where(near_hit(kk, i), nb[i, qs], a)
            if d:
                lsel[d, qs] = a
                along_l.append(send(lsel.at[d, qs], lrecv.at[NL - d, qs], dl=d))
            else:
                lrecv[0, qs] = a

    for cp in ask_y + list(rest.values()):
        cp.wait_recv()
    order = (0, 2, 1, 3)
    along_y = {}
    for q in order:
        ahead[q].wait_recv()
        along_y[q] = []
        for d in (2, 1, 3, 0):
            b = pick(lambda e: zhb[e, q], want(reqy[d], 1) % NH, NH, h)
            if d:
                bsend[d, q] = b
                along_y[q].append(send(bsend.at[d, q], brecv.at[NY - d, q], dy=d))
            else:
                brecv[0, q] = b

    for cp in along_l:
        cp.wait_recv()
    aop[...] = pick(lambda e: lrecv[e], (want(req[...], 0) // NC) % NL, NL, l)
    item = unpack_all(aop)
    centre = jnp.mean(item[0:3], axis=1, keepdims=True)
    ax, aal, ahs = item[0:3] - centre, item[3:6], 0.5 * item[6:7] * item[6:7]
    left[...] = metric(ax, ahs)[0]
    ea[...], fa[...] = moments(ax, aal)
    col[...] = column(1.5 * ahs)

    back_y = {}
    for q in order:
        for cp in along_y[q]:
            cp.wait_recv()
        bop[q] = pick(lambda e: brecv[e, q], want(req[...], 1) // NH, NY, y)
        item = unpack(bop, q)
        bx, bal, bhs = item[0:3] - centre, item[3:6], 0.5 * item[6:7] * item[6:7]
        js = pl.ds(q * TJ, TJ)
        right[:, js] = metric(bx, bhs)[1]
        eb[:, js], fb[:, js] = moments(bx, bal)
        rowj[:, js] = 1.5 * bhs
        pack(pb, q, finish(bx, bal, *block(q, True)))
        back_y[q] = [send(pb.at[q], yrecv.at[NY - d, q], dy=d) for d in (2, 1, 3)]
        yrecv[0, q] = pb[q]

    masks_h = []
    for d in range(NY):
        t = reqy[d]
        kk, mm, on = want(t, 0), want(t, 1), want(t, 2)
        self_pair = (mm == ((y + d) % NY) * NH + h) & (kk == (x * NL + l) * NC + c)
        mine = (on == 1) & (mm // NH == y) & jnp.logical_not(self_pair)
        masks_h.append([mine & (mm % NH == (h + e) % NH) for e in range(NH)])
    back_h = []

    def to_owner_h(q, es):
        for e in es:
            total = jnp.zeros((12, 128), f32)
            for d in range(NY):
                total = total + jnp.where(masks_h[d][e], yrecv[d, q], 0.0)
            if e:
                hsend[e, q] = total
                back_h.append(send(hsend.at[e, q], hrecv.at[NH - e, q], dh=e))
            else:
                hrecv[0, q] = total

    back_n = []
    for p, q in enumerate(order):
        rs = slice(p * TJ, p * TJ + TJ)
        pack(pa, p, finish(ax[:, rs], aal[:, rs], *row_block(p)))
        back_n.append([send(pa.at[p], nrecv.at[near_slot(dx, dc), p], dx=dx, dc=dc) for dx, dc in NEAR[1:]])
        nrecv[0, p] = pa[p]
        for cp in back_y[q]:
            cp.wait_recv()
        to_owner_h(q, (2,))
        if p:
            to_owner_h(order[p - 1], (1, 3))
    to_owner_h(order[3], (1, 3))

    for cp in ask_n:
        cp.wait_recv()
    masks_l = []
    for i in range(len(NEAR)):
        t = reqn[i]
        kk, on = want(t, 0), want(t, 2)
        mine = (on == 1) & (kk // (NL * NC) == x) & (kk % NC == c)
        masks_l.append([mine & ((kk // NC) % NL == (l + e) % NL) for e in range(NL)])
    back_l = []
    for p in range(NB):
        for cp in back_n[p]:
            cp.wait_recv()
        for e in (3, 2, 1, 0):
            total = jnp.zeros((12, 128), f32)
            for i in range(len(NEAR)):
                total = total + jnp.where(masks_l[i][e], nrecv[i, p], 0.0)
            if e:
                lsend[e, p] = total
                back_l.append(send(lsend.at[e, p], lback.at[NL - e, p], dl=e))
            else:
                lback[0, p] = total

    for q in range(NB):
        to_owner_h(q, (0,))
    for cp in sent:
        cp.wait_send()

    @pl.when(h == 2)
    def _():
        for cp in across.values():
            cp.wait_send()

    for d in (1, 3):
        @pl.when(h != NH - d)
        def _():
            for e, q in ways:
                if e == d:
                    ahead[q].wait_send()

    for cp in back_l + back_h:
        cp.wait_recv()
    for q in range(NB):
        pb[q] = ((hrecv[0, q] + hrecv[1, q]) + (hrecv[2, q] + hrecv[3, q])) + (
            (lback[0, q] + lback[1, q]) + (lback[2, q] + lback[3, q]))
    for t in range(8):
        lanes = slice(128 * t, 128 * t + 128)
        result[:, lanes] = sout[:, lanes] + pb[t // 2, pl.ds(t % 2, 6, stride=2), :]
    assert used[0] == N_COPIES


N_COPIES = 6 + 3 + 3 + 14 + 7 + 8 + 6 + 12 + 12 + 28 + 12 + 12


def local(positions, strengths, radii, pair_list, pair_count):
    vm, sm = pl.BlockSpec(memory_space=pltpu.VMEM), pl.BlockSpec(memory_space=pltpu.SMEM)
    hbm = pl.BlockSpec(memory_space=pltpu.HBM)
    V = pltpu.VMEM
    out = jax.ShapeDtypeStruct((6, G), f32)
    item, part = (NB, 14, 128), (NB, 12, 128)
    ask = (8, 128)
    result = pl.pallas_call(
        kernel,
        out_shape=out,
        in_specs=[hbm, hbm, hbm, sm, sm],
        out_specs=vm,
        scratch_shapes=[
            V((3, G), f32), V((3, G), f32), V((8, 128), f32),
            V(item, f32), V(ask, jnp.int32), V((NH,) + item, f32),
            V((NY,) + ask, jnp.int32), V((NL,) + ask, jnp.int32), V((8,) + ask, jnp.int32),
            V((8,) + item, f32), V((NL,) + item, f32), V((NL,) + item, f32),
            V((NY,) + item, f32), V((NY,) + item, f32), V(item, f32), V(item, f32),
            V(part, f32), V((NY,) + part, f32), V((NH,) + part, f32), V((NH,) + part, f32),
            V(part, f32), V((8,) + part, f32), V((NL,) + part, f32), V((NL,) + part, f32),
            V((48, G), bf16), V((48, G), bf16), V((G, 128), f32), V((1, G), f32),
            V((24, G), bf16), V((96, G), bf16), V((24, G), bf16), V((96, G), bf16),
            V((4, G, G), bf16), V((6, G), f32),
            pltpu.SemaphoreType.DMA((3,)), pltpu.SemaphoreType.DMA((N_COPIES,)), pltpu.SemaphoreType.DMA((N_COPIES,)),
        ],
        compiler_params=pltpu.CompilerParams(
            collective_id=0, has_side_effects=True, vmem_limit_bytes=64 * 2**20 - 2**16
        ),
        cost_estimate=pl.CostEstimate(flops=2 * G * G * 256, bytes_accessed=64 * G, transcendentals=2 * G * G),
        name="vortex_pairs",
    )(positions, strengths, radii.reshape(8, 128), pair_list, pair_count)
    return result[:3], result[3:]


def solution(mesh):
    placed = (
        P(None, ("row", "col")),
        P(None, ("row", "col")),
        P(("row", "col")),
        P(None, "row", "col", None),
        P("row", "col"),
    )
    return jax.shard_map(
        local,
        mesh=mesh,
        in_specs=placed,
        out_specs=(P(None, ("row", "col")), P(None, ("row", "col"))),
        check_vma=False,
    )
```

```python
import functools
import math

import jax
import jax.numpy as jnp
from jax import lax
from jax.experimental import pallas as pl
from jax.experimental.pallas import tpu as pltpu
from jax.sharding import PartitionSpec as P

G = 1024
MESH = pl.DeviceIdType.MESH
f32, bf16 = jnp.float32, jnp.bfloat16
TJ = 256
NB = G // TJ

NY, NH, NX, NL, NC = 4, 4, 4, 4, 2
NEAR = [(dx, dc) for dx in range(NX) for dc in range(NC)]


def coords():
    r, c = lax.axis_index("row"), lax.axis_index("col")
    return r // NH, r % NH, c // (NL * NC), (c // NC) % NL, c % NC


def at(dy=0, dh=0, dx=0, dl=0, dc=0):
    y, h, x, l, c = coords()
    row = ((y + dy) % NY) * NH + (h + dh) % NH
    col = (((x + dx) % NX) * NL + (l + dl) % NL) * NC + (c + dc) % NC
    return {"row": row, "col": col}


def split3(v):
    h = v.astype(bf16).astype(f32)
    rest = v - h
    m = rest.astype(bf16).astype(f32)
    return h, m, rest - m


def cross(p, q):
    return [p[1] * q[2] - p[2] * q[1], p[2] * q[0] - p[0] * q[2], p[0] * q[1] - p[1] * q[0]]


def rows_of(v, n):
    return [v[i : i + 1] for i in range(n)]


def unpack(ref, q):
    return jnp.concatenate([ref[q, pl.ds(s, 7, stride=2), :] for s in range(2)], axis=1)


def unpack_all(ref):
    return jnp.concatenate([unpack(ref, q) for q in range(NB)], axis=1)


def pack(ref, q, v):
    for s in range(2):
        ref[q, pl.ds(s, 6, stride=2), :] = v[:, s * 128 : (s + 1) * 128]


def metric(x, hs):
    n = x.shape[1]
    u = x[0:1] * x[0:1] + x[1:2] * x[1:2] + x[2:3] * x[2:3] + hs
    one, zero = jnp.ones((1, n), f32), jnp.zeros((3, n), f32)
    lh, lm, ll = split3(jnp.concatenate([-2.0 * x, u, one, zero], 0))
    rh, rm, rl = split3(jnp.concatenate([x, one, u, zero], 0))
    left = jnp.concatenate([lh, lh, lm, lm, lh, ll], 0).astype(bf16)
    right = jnp.concatenate([rh, rm, rh, rm, rl, rh], 0).astype(bf16)
    return left, right


def moments(x, al):
    e = jnp.concatenate([al] + cross(rows_of(x, 3), rows_of(al, 3)) + [jnp.zeros((2, x.shape[1]), f32)], 0)
    f = jnp.concatenate([e, x[0:1] * e, x[1:2] * e, x[2:3] * e], 0)
    return jnp.concatenate(split3(e), 0).astype(bf16), jnp.concatenate(split3(f), 0).astype(bf16)


def finish(x, al, sg, sh):
    xs, a = rows_of(x, 3), rows_of(al, 3)
    g0, g1 = rows_of(sg[0:3], 3), rows_of(sg[3:6], 3)
    sh = -5.0 * sh
    row = lambda p, q: sh[8 * p + q : 8 * p + q + 1]
    h0, h1 = [row(0, q) for q in range(3)], [row(0, 3 + q) for q in range(3)]
    at0 = [a[0] * row(1, q) + a[1] * row(2, q) + a[2] * row(3, q) for q in range(3)]
    at1 = [a[0] * row(1, 3 + q) + a[1] * row(2, 3 + q) + a[2] * row(3, 3 + q) for q in range(3)]
    ax = a[0] * xs[0] + a[1] * xs[1] + a[2] * xs[2]
    c0, c1, c2, c3 = cross(xs, g0), cross(xs, h0), cross(xs, at0), cross(a, g0)
    scale = 1.0 / (4.0 * math.pi)
    vel = [scale * (g1[i] - c0[i]) for i in range(3)]
    stretch = [-scale * (c3[i] + ax * (c1[i] - h1[i]) - c2[i] + at1[i]) for i in range(3)]
    return jnp.concatenate(vel + stretch, 0)


def dot(a, b, dims):
    return lax.dot_general(a, b, (dims, ((), ())), preferred_element_type=f32)


def halves(v):
    h = v.astype(bf16)
    return h, (v - h.astype(f32)).astype(bf16)


def kernels_of(left, right, si, sj):
    y = lax.rsqrt(dot(left, right, ((0,), (0,))))
    y2 = y * y
    p = y2 * y
    t = (si + sj) * y2
    return halves(p + p * t) + halves((p * y2) * (0.6 + t))


def fold(hi, lo, n):
    return (hi[:n] + hi[n : 2 * n] + hi[2 * n :]) + (lo[:n] + lo[n:])


def column(hs):
    return jnp.transpose(jnp.broadcast_to(hs, (128, hs.shape[1])))


def kernel(pos_in, stg_in, rad_in, plist, pcount, result,
           pos, stg, rad, own, req, zhb, reqy, reql, reqn, nb, lsel, lrecv, bsend, brecv, aop, bop,
           pb, yrecv, hsend, hrecv, pa, nrecv, lsend, lback,
           left, right, col, rowj, ea, fa, eb, fb, kept, sout, lsem, ssem, rsem):
    y, h, x, l, c = coords()
    bar = pltpu.get_barrier_semaphore()
    peers = (
        [dict(dh=1), dict(dh=3)]
        + [dict(dx=dx, dc=dc) for dx, dc in NEAR[1:]]
        + [dict(dl=d) for d in (1, 2, 3)]
        + [dict(dy=d) for d in (1, 2, 3)]
    )
    @pl.when(h == 0)
    def _():
        pl.semaphore_signal(bar, inc=1, device_id=at(dh=2), device_id_type=MESH)

    for o in peers:
        pl.semaphore_signal(bar, inc=1, device_id=at(**o), device_id_type=MESH)
    loads = [
        pltpu.make_async_copy(src, dst, lsem.at[i])
        for i, (src, dst) in enumerate([(pos_in, pos), (stg_in, stg), (rad_in, rad)])
    ]
    for cp in loads:
        cp.start()

    used = [0]
    sent = []

    def slot():
        used[0] += 1
        return used[0] - 1

    def prep(src, dst, i, r, **o):
        return pltpu.make_async_remote_copy(
            src_ref=src, dst_ref=dst, send_sem=ssem.at[i], recv_sem=rsem.at[r],
            device_id=at(**o), device_id_type=MESH)

    def send(src, dst, **o):
        i = slot()
        cp = prep(src, dst, i, i, **o)
        cp.start()
        sent.append(cp)
        return cp

    k, m, live = plist[0, 0, 0, 1], plist[1, 0, 0, 1], (pcount[0, 0] > 1).astype(jnp.int32)
    ri = lax.broadcasted_iota(jnp.int32, (8, 128), 0)
    req[...] = jnp.where(ri == 0, k, jnp.where(ri == 1, m, live))
    for cp in loads:
        cp.wait()
    for q in range(NB):
        js = slice(TJ * q, TJ * q + TJ)
        pack(own, q, jnp.concatenate([pos[:, js], stg[:, js]], axis=0))
        own[q, 12:14, :] = rad[2 * q : 2 * q + 2, :]

    item = unpack_all(own)
    own_x, own_al, own_r = item[0:3], item[3:6], item[6:7]
    own_x = own_x - jnp.mean(own_x, axis=1, keepdims=True)
    own_hs = 0.5 * own_r * own_r
    left[...], right[...] = metric(own_x, own_hs)
    ea[...], fa[...] = moments(own_x, own_al)
    rowj[...] = 1.5 * own_hs
    col[...] = column(1.5 * own_hs)

    def block(q, keep):
        js = pl.ds(q * TJ, TJ)
        si = jnp.concatenate([col[...]] * (TJ // 128), 1)
        parts = kernels_of(left[...], right[:, js], si, rowj[:, js])
        gh, gl, hh, hl = parts
        if keep:
            for i in range(4):
                kept[i, :, js] = parts[i]
        d = ((1,), (0,))
        sg = fold(dot(ea[...], gh, d), dot(ea[:16], gl, d), 8)
        sh = fold(dot(fa[...], hh, d), dot(fa[:64], hl, d), 32)
        return sg, sh

    def row_block(p):
        rs = pl.ds(p * TJ, TJ)
        d = ((1,), (1,))
        sg = fold(dot(eb[...], kept[0, rs, :], d), dot(eb[:16], kept[1, rs, :], d), 8)
        sh = fold(dot(fb[...], kept[2, rs, :], d), dot(fb[:64], kept[3, rs, :], d), 32)
        return sg, sh

    def own_block(q):
        js = slice(q * TJ, q * TJ + TJ)
        sout[:, js] = finish(own_x[:, js], own_al[:, js], *block(q, False))

    pl.semaphore_wait(bar, len(peers) + (h // 2) * (1 - h % 2))
    ways = ((1, 0), (3, 2), (1, 1), (3, 3))
    ahead, across = {}, {}
    for d, q in ways:
        i = slot()
        ahead[q] = prep(zhb.at[NH - d, pl.ds(q, 1)], zhb.at[2, pl.ds(q, 1)], i, i, dh=d)
        across[q] = prep(own.at[pl.ds(q, 1)], zhb.at[2, pl.ds(q, 1)], slot(), i, dh=2)

    @pl.when(h == 2)
    def _():
        for d, q in ways:
            across[q].start()

    def to_zh(q, n, d):
        return send(own.at[pl.ds(q, n)], zhb.at[NH - d, pl.ds(q, n)], dh=d)

    first = {(d, q): to_zh(q, 1, d) for d, q in ways}
    rest = {1: to_zh(2, 2, 1), 3: to_zh(0, 2, 3)}

    def near_slot(dx, dc):
        return ((NX - dx) % NX) * NC + dc

    ask_y = [send(req, reqy.at[NY - d], dy=d) for d in (1, 2, 3)]
    ask_l = [send(req, reql.at[NL - d], dl=d) for d in (1, 2, 3)]
    near = [
        [send(own.at[pl.ds(q, 2)], nb.at[near_slot(dx, dc), pl.ds(q, 2)], dx=dx, dc=dc) for dx, dc in NEAR[1:]]
        for q in (0, 2)
    ]
    ask_n = [send(req, reqn.at[near_slot(dx, dc)], dx=dx, dc=dc) for dx, dc in NEAR[1:]]
    zhb[0] = own[...]
    nb[0] = own[...]
    reql[0] = req[...]
    reqy[0] = req[...]
    reqn[0] = req[...]
    for q in range(NB):
        own_block(q)

    for d, q in ways:
        first[d, q].wait_recv()

        @pl.when(h != NH - d)
        def _():
            ahead[q].start()

    def want(tile, r):
        return tile[r : r + 1, :]

    def pick(buf, index, n, first):
        out = buf(0)
        for d in range(1, n):
            out = jnp.where(index == (first + d) % n, buf(d), out)
        return out

    def near_hit(kk, i):
        dx, dc = NEAR[i]
        return (kk // (NL * NC) == (x + dx) % NX) & (kk % NC == (c + dc) % NC)

    for cp in ask_l:
        cp.wait_recv()
    along_l = []
    for half in range(2):
        for cp in near[half]:
            cp.wait_recv()
        qs = pl.ds(2 * half, 2)
        for d in (1, 2, 3, 0):
            kk = want(reql[d], 0)
            a = nb[0, qs]
            for i in range(1, len(NEAR)):
                a = jnp.where(near_hit(kk, i), nb[i, qs], a)
            if d:
                lsel[d, qs] = a
                along_l.append(send(lsel.at[d, qs], lrecv.at[NL - d, qs], dl=d))
            else:
                lrecv[0, qs] = a

    for cp in ask_y + list(rest.values()):
        cp.wait_recv()
    order = (0, 2, 1, 3)
    along_y = {}
    for q in order:
        ahead[q].wait_recv()
        along_y[q] = []
        for d in (2, 1, 3, 0):
            b = pick(lambda e: zhb[e, q], want(reqy[d], 1) % NH, NH, h)
            if d:
                bsend[d, q] = b
                along_y[q].append(send(bsend.at[d, q], brecv.at[NY - d, q], dy=d))
            else:
                brecv[0, q] = b

    for cp in along_l:
        cp.wait_recv()
    aop[...] = pick(lambda e: lrecv[e], (want(req[...], 0) // NC) % NL, NL, l)
    item = unpack_all(aop)
    centre = jnp.mean(item[0:3], axis=1, keepdims=True)
    ax, aal, ahs = item[0:3] - centre, item[3:6], 0.5 * item[6:7] * item[6:7]
    left[...] = metric(ax, ahs)[0]
    ea[...], fa[...] = moments(ax, aal)
    col[...] = column(1.5 * ahs)

    back_y = {}
    for q in order:
        for cp in along_y[q]:
            cp.wait_recv()
        bop[q] = pick(lambda e: brecv[e, q], want(req[...], 1) // NH, NY, y)
        item = unpack(bop, q)
        bx, bal, bhs = item[0:3] - centre, item[3:6], 0.5 * item[6:7] * item[6:7]
        js = pl.ds(q * TJ, TJ)
        right[:, js] = metric(bx, bhs)[1]
        eb[:, js], fb[:, js] = moments(bx, bal)
        rowj[:, js] = 1.5 * bhs
        pack(pb, q, finish(bx, bal, *block(q, True)))
        back_y[q] = [send(pb.at[q], yrecv.at[NY - d, q], dy=d) for d in (2, 1, 3)]
        yrecv[0, q] = pb[q]

    masks_h = []
    for d in range(NY):
        t = reqy[d]
        kk, mm, on = want(t, 0), want(t, 1), want(t, 2)
        self_pair = (mm == ((y + d) % NY) * NH + h) & (kk == (x * NL + l) * NC + c)
        mine = (on == 1) & (mm // NH == y) & jnp.logical_not(self_pair)
        masks_h.append([mine & (mm % NH == (h + e) % NH) for e in range(NH)])
    back_h = []

    def to_owner_h(q, es):
        for e in es:
            total = jnp.zeros((12, 128), f32)
            for d in range(NY):
                total = total + jnp.where(masks_h[d][e], yrecv[d, q], 0.0)
            if e:
                hsend[e, q] = total
                back_h.append(send(hsend.at[e, q], hrecv.at[NH - e, q], dh=e))
            else:
                hrecv[0, q] = total

    back_n = []
    for p, q in enumerate(order):
        rs = slice(p * TJ, p * TJ + TJ)
        pack(pa, p, finish(ax[:, rs], aal[:, rs], *row_block(p)))
        back_n.append([send(pa.at[p], nrecv.at[near_slot(dx, dc), p], dx=dx, dc=dc) for dx, dc in NEAR[1:]])
        nrecv[0, p] = pa[p]
        for cp in back_y[q]:
            cp.wait_recv()
        to_owner_h(q, (2,))
        if p:
            to_owner_h(order[p - 1], (1, 3))
    to_owner_h(order[3], (1, 3))

    for cp in ask_n:
        cp.wait_recv()
    masks_l = []
    for i in range(len(NEAR)):
        t = reqn[i]
        kk, on = want(t, 0), want(t, 2)
        mine = (on == 1) & (kk // (NL * NC) == x) & (kk % NC == c)
        masks_l.append([mine & ((kk // NC) % NL == (l + e) % NL) for e in range(NL)])
    back_l = []
    for p in range(NB):
        for cp in back_n[p]:
            cp.wait_recv()
        for e in (3, 2, 1, 0):
            total = jnp.zeros((12, 128), f32)
            for i in range(len(NEAR)):
                total = total + jnp.where(masks_l[i][e], nrecv[i, p], 0.0)
            if e:
                lsend[e, p] = total
                back_l.append(send(lsend.at[e, p], lback.at[NL - e, p], dl=e))
            else:
                lback[0, p] = total

    for q in range(NB):
        to_owner_h(q, (0,))
    for cp in sent:
        cp.wait_send()

    @pl.when(h == 2)
    def _():
        for cp in across.values():
            cp.wait_send()

    for d in (1, 3):
        @pl.when(h != NH - d)
        def _():
            for e, q in ways:
                if e == d:
                    ahead[q].wait_send()

    for cp in back_l:
        cp.wait_recv()
    for q in range(NB):
        pa[q] = (lback[0, q] + lback[1, q]) + (lback[2, q] + lback[3, q])
    for t in range(8):
        lanes = slice(128 * t, 128 * t + 128)
        sout[:, lanes] = sout[:, lanes] + pa[t // 2, pl.ds(t % 2, 6, stride=2), :]
    for cp in back_h:
        cp.wait_recv()
    for q in range(NB):
        pb[q] = (hrecv[0, q] + hrecv[1, q]) + (hrecv[2, q] + hrecv[3, q])
    for t in range(8):
        lanes = slice(128 * t, 128 * t + 128)
        result[:, lanes] = sout[:, lanes] + pb[t // 2, pl.ds(t % 2, 6, stride=2), :]
    assert used[0] == N_COPIES


N_COPIES = 6 + 3 + 3 + 14 + 7 + 8 + 6 + 12 + 12 + 28 + 12 + 12


def local(positions, strengths, radii, pair_list, pair_count):
    vm, sm = pl.BlockSpec(memory_space=pltpu.VMEM), pl.BlockSpec(memory_space=pltpu.SMEM)
    hbm = pl.BlockSpec(memory_space=pltpu.HBM)
    V = pltpu.VMEM
    out = jax.ShapeDtypeStruct((6, G), f32)
    item, part = (NB, 14, 128), (NB, 12, 128)
    ask = (8, 128)
    result = pl.pallas_call(
        kernel,
        out_shape=out,
        in_specs=[hbm, hbm, hbm, sm, sm],
        out_specs=vm,
        scratch_shapes=[
            V((3, G), f32), V((3, G), f32), V((8, 128), f32),
            V(item, f32), V(ask, jnp.int32), V((NH,) + item, f32),
            V((NY,) + ask, jnp.int32), V((NL,) + ask, jnp.int32), V((8,) + ask, jnp.int32),
            V((8,) + item, f32), V((NL,) + item, f32), V((NL,) + item, f32),
            V((NY,) + item, f32), V((NY,) + item, f32), V(item, f32), V(item, f32),
            V(part, f32), V((NY,) + part, f32), V((NH,) + part, f32), V((NH,) + part, f32),
            V(part, f32), V((8,) + part, f32), V((NL,) + part, f32), V((NL,) + part, f32),
            V((48, G), bf16), V((48, G), bf16), V((G, 128), f32), V((1, G), f32),
            V((24, G), bf16), V((96, G), bf16), V((24, G), bf16), V((96, G), bf16),
            V((4, G, G), bf16), V((6, G), f32),
            pltpu.SemaphoreType.DMA((3,)), pltpu.SemaphoreType.DMA((N_COPIES,)), pltpu.SemaphoreType.DMA((N_COPIES,)),
        ],
        compiler_params=pltpu.CompilerParams(
            collective_id=0, has_side_effects=True, vmem_limit_bytes=64 * 2**20 - 2**16
        ),
        cost_estimate=pl.CostEstimate(flops=2 * G * G * 256, bytes_accessed=64 * G, transcendentals=2 * G * G),
        name="vortex_pairs",
    )(positions, strengths, radii.reshape(8, 128), pair_list, pair_count)
    return result[:3], result[3:]


def solution(mesh):
    placed = (
        P(None, ("row", "col")),
        P(None, ("row", "col")),
        P(("row", "col")),
        P(None, "row", "col", None),
        P("row", "col"),
    )
    return jax.shard_map(
        local,
        mesh=mesh,
        in_specs=placed,
        out_specs=(P(None, ("row", "col")), P(None, ("row", "col"))),
        check_vma=False,
    )
```
